256 devices in a mesh: lon: 16 (over x_hi, z), lat: 8 (over y, x_lo), ch: 2 (over core).
Axes of the slice: x: 4 (x_hi: 2, x_lo: 2; x = x_hi * 2 + x_lo), y: 4, z: 8, core: 2. Of those that a mesh axis runs over, the one named last changes fastest.
Arguments:
- fields: bfloat16 [69, 512, 2048], P(None, 'lat', 'lon'), may hold values from -6 to 6
- conv_weight: bfloat16 [128, 9, 69], P('ch'), may hold values from -0.25 to 0.25
- embed_weight: bfloat16 [128, 16384], replicated, may hold values from -0.125 to 0.125
- token_grads: bfloat16 [16, 8, 512, 1024], P('lon', 'lat'), may hold values from -0.0234375 to 0.0234375
Outputs:
- embedded: bfloat16 [16, 8, 512, 1024], P('lon', 'lat', None, 'ch')
- conv_gradient: float32 [128, 9, 69], P('ch')
- embed_gradient: float32 [128, 16384], P('ch', ('lon', 'lat'))
The draws below stay inside these ranges and needn't reach their ends.
All inputs are finite; a program needn't handle non-finite values.
Results may differ from the reference program's by a relative error of at most 0.0049.
Values may be sent and summed in bfloat16 or wider, within the bound.
A program may use at most 128 MiB of HBM per device.

```python
import jax
import jax.numpy as jnp
from jax import lax

C_IN = 69
C1 = 128
E = 1024
R_DEV = 64
NLAT = 512
NLON = 2048
NPC = 512


def shard_levels(key, extent, pieces, smallest, top_value):
    level = 1.0
    for dim, blocks in pieces:
        steps = jax.random.uniform(jax.random.fold_in(jax.random.fold_in(key, 6), dim), (blocks,), jnp.float32, smallest / len(pieces), top_value / len(pieces))
        level = level * jnp.repeat(jnp.exp(steps), extent[dim] // blocks).reshape((-1,) + (1,) * (len(extent) - 1 - dim))
    return level


def scatter_about(key, dims, width, reach, shards=(), kind=jnp.bfloat16):
    array = jax.random.normal(key, dims, jnp.float32) * width
    if len(shards) > 0:
        array = shard_levels(key, dims, shards, -0.22, 0.18) * array
    return jnp.clip(array, min=-reach, max=reach).astype(kind)


def setup_inputs(seed: int = 0) -> dict:
    key_list = jax.random.split(jax.random.key(seed), 5)
    return {
        "fields": scatter_about(key_list[0], (C_IN, NLAT, NLON), 1.0, 6.0, ((1, 8), (2, 16))),
        "conv_weight": scatter_about(key_list[1], (C1, 9, C_IN), (9 * C_IN) ** -0.5, 0.25, ((0, 2),)),
        "embed_weight": scatter_about(key_list[2], (C1, 16 * E), (16 * C1) ** -0.5, 0.125),
        "token_grads": scatter_about(key_list[3], (R_DEV // 4, NLAT // R_DEV, NPC, E), ((NLAT * NLON // 16) ** -0.5), 0.0234375, ((0, 16), (1, 8))),
    }


def pad_poles(fields):
    half_loop = fields.shape[2] // 2
    top_row = jnp.roll(fields[:, :1, :], half_loop, axis=2)
    bottom_row = jnp.roll(fields[:, -1:, :], half_loop, axis=2)
    stacked = jnp.concatenate([top_row, fields, bottom_row], axis=1)
    return jnp.concatenate([stacked[:, :, -1:], stacked, stacked[:, :, :1]], axis=2)

def convolve(weights, extended, row_count, col_count):
    total = jnp.zeros((weights.shape[0], row_count * col_count), jnp.float32)
    for position in range(9):
        row_shift, col_shift = divmod(position, 3)
        window = extended[:, row_shift:row_shift + row_count, col_shift:col_shift + col_count]
        total = total + jnp.dot(weights[:, position, :], window.reshape(extended.shape[0], row_count * col_count), preferred_element_type=jnp.float32)
    return total

def weight_terms(preact_grad, extended, row_count, col_count):
    terms = []
    for position in range(9):
        row_shift, col_shift = divmod(position, 3)
        window = extended[:, row_shift:row_shift + row_count, col_shift:col_shift + col_count]
        window = window.reshape(extended.shape[0], row_count * col_count)
        terms.append(lax.dot_general(preact_grad, window, (((1,), (1,)), ((), ())), preferred_element_type=jnp.float32))
    return jnp.stack(terms, axis=1)

def patchify(hidden, channels, row_count, col_count):
    shaped = hidden.reshape(channels, row_count // 4, 4, col_count // 4, 4)
    return shaped.transpose(1, 3, 0, 2, 4).reshape(row_count // 4 * (col_count // 4), channels * 16)

def unpatchify(patch_grad, channels, row_count, col_count):
    shaped = patch_grad.reshape(row_count // 4, col_count // 4, channels, 4, 4)
    return shaped.transpose(2, 0, 3, 1, 4).reshape(channels, row_count * col_count)

def reference(fields, conv_weight, embed_weight, token_grads):
    padded = pad_poles(fields)
    embed_matrix = embed_weight.reshape(C1 * 16, E)

    def band_step(running, band_index):
        conv_sum, embed_sum = running
        offset = (band_index * R_DEV).astype(jnp.int32)
        extended = lax.dynamic_slice_in_dim(padded, offset, R_DEV + 2, 1)
        preact = convolve(conv_weight, extended, R_DEV, NLON)
        hidden, gelu_back = jax.vjp(jax.nn.gelu, preact)
        patch_rows = patchify(hidden.astype(jnp.bfloat16), C1, R_DEV, NLON)
        embedded = jnp.dot(patch_rows, embed_matrix, preferred_element_type=jnp.float32).astype(jnp.bfloat16)
        token_rows = lax.dynamic_slice_in_dim(token_grads, band_index.astype(jnp.int32), 1, 1).reshape(-1, E)
        patch_grad = lax.dot_general(token_rows, embed_matrix, (((1,), (1,)), ((), ())), preferred_element_type=jnp.float32)
        embed_sum = embed_sum + lax.dot_general(patch_rows, token_rows, (((0,), (0,)), ((), ())), preferred_element_type=jnp.float32)
        preact_grad = gelu_back(unpatchify(patch_grad, C1, R_DEV, NLON))[0].astype(jnp.bfloat16)
        conv_sum = conv_sum + weight_terms(preact_grad, extended, R_DEV, NLON)
        return ((conv_sum, embed_sum), embedded.reshape(R_DEV // 4, NPC, E))
    initial = (jnp.zeros((C1, 9, C_IN), jnp.float32), jnp.zeros((C1 * 16, E), jnp.float32))
    finals, stacked = lax.scan(band_step, initial, jnp.arange(NLAT // R_DEV, dtype=jnp.int32))
    conv_sum, embed_sum = finals
    return (stacked.transpose(1, 0, 2, 3), conv_sum, embed_sum.reshape(C1, 16 * E))
```

```python
import functools

import jax
import jax.numpy as jnp
from jax import lax
from jax.experimental import pallas as pl
from jax.experimental.pallas import tpu as pltpu
from jax.sharding import PartitionSpec as P

BF = jnp.bfloat16
F32 = jnp.float32
MESH = pl.DeviceIdType.MESH
CP = 80
NN = (((1,), (0,)), ((), ()))
NT = (((1,), (1,)), ((), ()))


def dot(x, y, dims=NN):
    return lax.dot_general(x, y, dims, preferred_element_type=F32)


def one_hot(target, rows):
    index = lax.broadcasted_iota(jnp.int32, (rows, target.shape[1]), 0)
    return jnp.where(index == target, 1.0, 0.0).astype(BF)


def kernel(
    t_ref, wc_ref, w_ref, tg_ref,
    emb_out, eg_out, cg_out,
    slab, halo_l, halo_r, got_l, got_r, pack_l, pack_r,
    wc, wv, tgo, tgp, src, p1, xs, hid, hidp, hidt, dgelu, emb,
    egb, ego, ra, sbf, sbb, rb, scf, scb, rc,
    cga, cgp, scg, rcg, l0, rl, l1, agb, full,
    loc, tg_s, tg_r, ha_s, ha_r, pk_s, pk_r, wc_s, wc_r, em_s, em_r, tf_s, tf_r, hp_s, hp_r,
    a_s, a_r, b_s, b_r, c_s, c_r, q_s, q_r, d_s, d_r, e_s, e_r, f_s, f_r,
):
    lon = lax.axis_index("lon")
    lat = lax.axis_index("lat")
    ch = lax.axis_index("ch")
    hi = lon // 8
    lo = lax.rem(lon, 8)
    y = lat // 2
    xlo = lax.rem(lat, 2)
    other = 1 - ch

    def remote(source, target, send, recv, to_lon, to_lat, to_ch):
        return pltpu.make_async_remote_copy(
            src_ref=source, dst_ref=target, send_sem=send, recv_sem=recv,
            device_id=(to_lon, to_lat, to_ch), device_id_type=MESH,
        )

    slab_copy = pltpu.make_async_copy(t_ref.at[pl.ds(31 * ch, 33)], slab.at[pl.ds(other, 33)], loc.at[0])
    slab_copy.start()

    def halo_copies(row, to_lat, base):
        out = []
        for n, (shift, target) in enumerate(((0, slab.at[33 * ch]), (1, halo_l), (15, halo_r))):
            to = lax.rem(base + shift, 16)
            out.append(remote(t_ref.at[row], target, ha_s.at[n], ha_r.at[n], to, to_lat, ch))
        return out

    inner = halo_copies(63 * other, lat + 1 - 2 * ch, lon)
    polar_s = []
    for n, (shift, target) in enumerate(((0, slab.at[33 * ch]), (1, halo_l), (15, halo_r))):
        to = lax.rem(lon + 8 + shift, 16)
        polar_s.append(remote(t_ref.at[63 * ch], target, ha_s.at[3 + n], ha_r.at[n], to, lat, ch))
    has_inner = lat != 7 * other
    has_polar = lat == 7 * ch

    @pl.when(has_inner)
    def _():
        for c in inner:
            c.start()

    @pl.when(has_polar)
    def _():
        for c in polar_s:
            c.start()

    wc_local = pltpu.make_async_copy(wc_ref, wc.at[:, pl.ds(pl.multiple_of(64 * ch, 64), 64), :], loc.at[1])
    wc_local.start()
    wc_remote = remote(
        wc_ref, wc.at[:, pl.ds(pl.multiple_of(64 * ch, 64), 64), :], wc_s, wc_r, lon, lat, other
    )
    wc_remote.start()

    tg_copies = []
    for i in range(8):
        to = 8 * ch + lax.rem(lo + i, 8)
        tg_copies.append(
            remote(
                tg_ref.at[pl.ds(pl.multiple_of(32 * to, 32), 32)],
                tgo.at[pl.ds(pl.multiple_of(32 * lo, 32), 32)],
                tg_s.at[i], tg_r.at[i], to, lat, hi,
            )
        )
    tg_self = pltpu.make_async_copy(
        tg_ref.at[pl.ds(pl.multiple_of(32 * lon, 32), 32)],
        tgo.at[pl.ds(pl.multiple_of(32 * lo, 32), 32)],
        tg_r.at[0],
    )

    for i in (4, 3, 5, 2, 6, 1, 7):
        tg_copies[i].start()

    @pl.when(ch == hi)
    def _():
        tg_self.start()

    @pl.when(ch != hi)
    def _():
        tg_copies[0].start()

    w_copies = [
        pltpu.make_async_copy(w_ref.at[:, pl.ds(1024 * s, 1024)], wv.at[s], loc.at[2 + s]) for s in range(16)
    ]
    for c in w_copies:
        c.start()

    j = lax.broadcasted_iota(jnp.int32, (1, 768), 1)
    column = 4 * (j % 32) + j // 128 - 1
    target = jnp.where((column >= 0) & (column < 128), column + 128 * ((j % 128) // 32), -1)
    p1[...] = one_hot(target, 512)
    xs[:, 480:496, :] = jnp.zeros((6, 16, 256), BF)
    cga[...] = jnp.zeros_like(cga)

    slab_copy.wait()
    lane = lax.broadcasted_iota(jnp.int32, (CP, 128), 1)
    left = jnp.zeros((CP, 128), F32)
    right = jnp.zeros((CP, 128), F32)
    for m in range(33):
        row = slab[other + m].astype(F32)
        if m:
            row = pltpu.roll(row, m, 1)
        left = jnp.where(lane == (m + 127) % 128, row, left)
        right = jnp.where(lane == m, row, right)
    pack_l[...] = left.astype(BF)
    pack_r[...] = right.astype(BF)
    pk0 = remote(pack_l, got_l, pk_s.at[0], pk_r.at[0], lax.rem(lon + 1, 16), lat, ch)
    pk1 = remote(pack_r, got_r, pk_s.at[1], pk_r.at[1], lax.rem(lon + 15, 16), lat, ch)
    pk0.start()
    pk1.start()

    for c in inner:
        c.wait_recv()

    def gather_rows(u, _):
        for half in range(2):
            for k in range(4):
                src[u, pl.ds(CP * half, CP), 128 * k : 128 * k + 128] = slab[16 * half + 4 * k + u]
        return 0

    lax.fori_loop(0, 6, gather_rows, 0)
    pk0.wait_recv()
    pk1.wait_recv()
    edges = jnp.concatenate([got_l[...], got_r[...], halo_l[...], halo_r[...]], axis=1)
    j2 = lax.broadcasted_iota(jnp.int32, (1, 256), 1)
    side = j2 // 128
    at_edge = (j2 % 32) == 31 * side

    def depth(u, _):
        res = dot(src[u], p1[...])
        for half in range(2):
            row = 16 * half + u + 4 * ((j2 % 128) // 32)
            m = row - other
            own = jnp.where(side == 0, (m + 127) % 128, 128 + m)
            want = jnp.where(row == 33 * ch, jnp.where(side == 0, 256 + 127, 384), own)
            fill = dot(edges, one_hot(jnp.where(at_edge, want, -1), 512))
            part = res[CP * half : CP * half + CP]
            lanes = slice(128 * half, 128 * half + 128)
            xs[u, 0:CP, lanes] = (part[:, 0:128] + fill[:, 0:128]).astype(BF)
            for v in range(1, 5):
                xs[u, CP * v : CP * v + CP, lanes] = part[:, 128 * v : 128 * v + 128].astype(BF)
            xs[u, CP * 5 : CP * 6, lanes] = (part[:, 640:768] + fill[:, 128:256]).astype(BF)
        return 0

    lax.fori_loop(0, 6, depth, 0)

    wc_local.wait()
    wc_remote.wait_recv()

    def conv(s, _):
        a = s // 4
        first = pl.multiple_of(CP * (s % 4), 16)
        v = jnp.zeros((128, 256), F32)
        for da in range(3):
            v = v + dot(wc[da], xs[a + da, pl.ds(first, 256), :])
        root = 0.7978845608028654
        square = v * v
        th = jnp.tanh(root * v * (1.0 + 0.044715 * square))
        half = 0.5 * (1.0 + th)
        slope = half + 0.5 * v * (1.0 - th * th) * (root * (1.0 + 3 * 0.044715 * square))
        h = (v * half).astype(BF)
        dgelu[s] = slope
        hid[s] = h.reshape(2, 64, 256)
        hidt[:, pl.ds(pl.multiple_of(128 * s, 128), 128)] = h.T
        return 0

    lax.fori_loop(0, 16, conv, 0)
    hp = remote(hid.at[:, other], hidp, hp_s, hp_r, lon, lat, other)
    hp.start()

    for c in w_copies:
        c.wait()

    def embed(n, _):
        columns = pl.ds(pl.multiple_of(256 * n, 256), 256)
        part = jnp.zeros((256, 256), F32)
        for s in range(16):
            part = part + dot(hidt[:, 128 * s : 128 * s + 128], wv[s, :, columns])
        emb[n // 2, :, pl.ds(pl.multiple_of(256 * (n % 2), 256), 256)] = part.astype(BF)
        return 0

    lax.fori_loop(0, 4, embed, 0)
    emb_copies = {}
    for i in (4, 3, 5, 2, 6, 1, 7, 0):
        r = lax.rem(lo + i, 8)
        for g in range(2):
            emb_copies[i, g] = remote(
                emb.at[g, pl.ds(pl.multiple_of(32 * r, 32), 32)],
                emb_out.at[pl.ds(pl.multiple_of(32 * lon, 32), 32)],
                em_s.at[2 * i + g], em_r.at[2 * i + hi], 8 * ch + r, lat, g,
            )
            if i:
                emb_copies[i, g].start()
            else:
                mine = (ch == hi) & (ch == g)

                @pl.when(mine)
                def _(g=g):
                    pltpu.make_async_copy(
                        emb.at[g, pl.ds(pl.multiple_of(32 * lo, 32), 32)],
                        emb_out.at[pl.ds(pl.multiple_of(32 * lon, 32), 32)],
                        em_r.at[hi],
                    ).start()

                @pl.when(jnp.logical_not(mine))
                def _(g=g):
                    emb_copies[0, g].start()

    forwards = []
    for n, i in enumerate((0, 1, 7, 2, 6, 3, 5, 4)):
        tg_copies[i].wait_recv()
        rows = pl.ds(pl.multiple_of(32 * lax.rem(lo + 8 - i, 8), 32), 32)
        c = remote(tgo.at[rows], tgp.at[rows], tf_s.at[n], tf_r.at[n], lon, lat, other)
        c.start()
        forwards.append(c)
    hp.wait_recv()
    for c in forwards:
        c.wait_recv()

    def a_copy(cc, n):
        rows = pl.ds(pl.multiple_of(256 * cc, 256), 256)
        return remote(
            egb.at[n - 1, rows], ra.at[n - 1, rows], a_s.at[cc, n - 1], a_r.at[cc, n - 1],
            lon, lax.rem(lat + 2 * n, 8), ch,
        )

    def eg_part(cc, n):
        columns = pl.ds(pl.multiple_of(256 * lax.rem(y + n, 4), 256), 256)
        mine = hid[pl.ds(4 * cc, 4), ch].reshape(256, 256)
        theirs = hidp[pl.ds(4 * cc, 4)].reshape(256, 256)
        return dot(mine, tgo[:, columns]) + dot(theirs, tgp[:, columns])

    def stage_a(cc, _):
        rows = pl.ds(pl.multiple_of(256 * cc, 256), 256)
        for n in (2, 1, 3):
            egb[n - 1, rows] = eg_part(cc, n).astype(BF)
            a_copy(cc, n).start()
        ego[rows] = eg_part(cc, 0)
        return 0

    lax.fori_loop(0, 4, stage_a, 0)

    def conv_grad(a, _):
        hg = dot(wv[pl.ds(4 * a, 4)].reshape(512, 1024), tgo[...], NT)
        pg = (hg * dgelu[pl.ds(4 * a, 4)].reshape(512, 256)).astype(BF)
        for b in range(4):
            for da in range(3):
                cga[da] += dot(pg[128 * b : 128 * b + 128], xs[a + da, CP * b : CP * b + 256, :], NT)
        return 0

    lax.fori_loop(0, 4, conv_grad, 0)
    theirs = pl.ds(pl.multiple_of(64 * other, 64), 64)
    q_copy = remote(cga.at[:, theirs, :], cgp, q_s, q_r, lon, lat, other)
    q_copy.start()

    def b_copy(cc):
        rows = pl.ds(pl.multiple_of(256 * cc, 256), 256)
        return remote(sbb.at[other_x, rows], rb.at[rows], b_s.at[cc], b_r.at[cc], lon, lat + 1 - 2 * xlo, ch)

    other_x = 1 - xlo

    def stage_b(cc, _):
        rows = pl.ds(pl.multiple_of(256 * cc, 256), 256)
        total = ego[rows]
        for n in (1, 3, 2):
            a_copy(cc, n).wait_recv()
            total = total + ra[n - 1, rows].astype(F32)
        for g in range(2):
            piece = total[:, 128 * g : 128 * g + 128]
            sbf[g, rows] = piece
            sbb[g, rows] = piece.astype(BF)
        b_copy(cc).start()
        return 0

    def c_copy(s):
        i = lax.rem(s - lon + 16, 16)
        return remote(scb.at[s], rc.at[i], c_s.at[i], c_r.at[i], s, lat, ch)

    def stage_c(cc, _):
        rows = pl.ds(pl.multiple_of(256 * cc, 256), 256)
        b_copy(cc).wait_recv()
        total = (sbf[xlo, rows] + rb[rows].astype(F32)).reshape(4, 64, 128)
        scf[pl.ds(4 * cc, 4)] = total
        scb[pl.ds(4 * cc, 4)] = total.astype(BF)
        for k in range(4):
            s = 4 * cc + k

            @pl.when(s != lon)
            def _():
                c_copy(s).start()

        return 0

    def d_copy(i):
        to = lax.rem(lon + i, 16)
        return remote(scg.at[to], rcg.at[i], d_s.at[i], d_r.at[i], to, lat, ch)

    def e_copy(i):
        return remote(l0, rl.at[lat], e_s.at[i], e_r.at[i], lon, lax.rem(lat + i, 8), ch)

    def f_copy(i):
        return remote(l1, agb.at[lon], f_s.at[i], f_r.at[i], lax.rem(lon + i, 16), lat, ch)

    q_copy.wait_recv()
    total = cga[:, pl.ds(pl.multiple_of(64 * ch, 64), 64), :] + cgp[...]
    for n in range(16):
        ob, half = n // 2, n % 2
        scg[n] = total[:, 8 * ob : 8 * ob + 8, 128 * half : 128 * half + 128]
    for i in range(1, 16):
        d_copy(i).start()

    stage_b(0, 0)

    total = scg[lon]
    for i in range(1, 16):
        d_copy(i).wait_recv()
        total = total + rcg[i]
    l0[...] = total
    rl[lat] = total
    for i in range(1, 8):
        e_copy(i).start()

    stage_b(1, 0)
    stage_c(0, 0)

    for i in range(1, 8):
        e_copy(i).wait_recv()
    total = rl[0]
    for i in range(1, 8):
        total = total + rl[i]
    l1[...] = total
    agb[lon] = total
    for i in range(1, 16):
        f_copy(i).start()

    stage_b(2, 0)
    stage_c(1, 0)
    stage_b(3, 0)
    stage_c(2, 0)

    for i in range(1, 16):
        f_copy(i).wait_recv()
    for n in range(16):
        ob, half = n // 2, n % 2
        full[:, 8 * ob : 8 * ob + 8, 128 * half : 128 * half + 128] = agb[n]
    for da in range(3):
        for db in range(3):
            cg_out[3 * da + db] = full[da, :, CP * db : CP * db + 69]

    stage_c(3, 0)
    total = scf[lon]
    for i in range(1, 16):
        remote(scb.at[0], rc.at[i], c_s.at[i], c_r.at[i], lon, lat, other).wait_recv()
        total = total + rc[i].astype(F32)
    eg_out[...] = total

    for i in range(8):
        for g in range(2):
            remote(
                emb.at[0, pl.ds(0, 32)], emb_out.at[pl.ds(0, 32)],
                em_s.at[0], em_r.at[2 * i + g], lon, lat, other,
            ).wait_recv()

    @pl.when(has_inner)
    def _():
        for c in inner:
            c.wait_send()

    @pl.when(has_polar)
    def _():
        for c in polar_s:
            c.wait_send()

    wc_remote.wait_send()
    for i in range(1, 8):
        tg_copies[i].wait_send()

    @pl.when(ch != hi)
    def _():
        tg_copies[0].wait_send()

    pk0.wait_send()
    pk1.wait_send()
    hp.wait_send()
    q_copy.wait_send()
    for c in forwards:
        c.wait_send()
    for (i, g), c in emb_copies.items():
        if i:
            c.wait_send()
        else:

            @pl.when(jnp.logical_not((ch == hi) & (ch == g)))
            def _(c=c):
                c.wait_send()

    for cc in range(4):
        for n in (1, 2, 3):
            a_copy(cc, n).wait_send()
        b_copy(cc).wait_send()
    for i in range(1, 16):
        remote(scb.at[0], rc.at[i], c_s.at[i], c_r.at[i], lon, lat, other).wait_send()
        d_copy(i).wait_send()
        f_copy(i).wait_send()
    for i in range(1, 8):
        e_copy(i).wait_send()


def step(t, wc, w, tg):
    vm = pltpu.VMEM
    sem = pltpu.SemaphoreType.DMA
    scratch = [
        vm((34, CP, 128), BF), vm((CP, 128), BF), vm((CP, 128), BF), vm((CP, 128), BF), vm((CP, 128), BF),
        vm((CP, 128), BF), vm((CP, 128), BF),
        vm((3, 128, 256), BF), vm((16, 128, 1024), BF), vm((256, 1024), BF), vm((256, 1024), BF),
        vm((6, 2 * CP, 512), BF), vm((512, 768), BF), vm((6, 496, 256), BF),
        vm((16, 2, 64, 256), BF), vm((16, 64, 256), BF), vm((256, 2048), BF), vm((16, 128, 256), F32),
        vm((2, 256, 512), BF),
        vm((3, 1024, 256), BF), vm((1024, 256), F32), vm((3, 1024, 256), BF),
        vm((2, 1024, 128), F32), vm((2, 1024, 128), BF), vm((1024, 128), BF),
        vm((16, 64, 128), F32), vm((16, 64, 128), BF), vm((16, 64, 128), BF),
        vm((3, 128, 256), F32), vm((3, 64, 256), F32), vm((16, 3, 8, 128), F32), vm((16, 3, 8, 128), F32),
        vm((3, 8, 128), F32), vm((8, 3, 8, 128), F32), vm((3, 8, 128), F32), vm((16, 3, 8, 128), F32),
        vm((3, 64, 256), F32),
        sem((18,)), sem((8,)), sem((8,)), sem((6,)), sem((3,)), sem((2,)), sem((2,)), sem, sem,
        sem((16,)), sem((16,)), sem((8,)), sem((8,)), sem, sem,
        sem((4, 3)), sem((4, 3)), sem((4,)), sem((4,)), sem((16,)), sem((16,)), sem, sem,
        sem((16,)), sem((16,)), sem((8,)), sem((8,)), sem((16,)), sem((16,)),
    ]
    any_ = pl.BlockSpec(memory_space=pl.ANY)
    inside = pl.BlockSpec(memory_space=pltpu.VMEM)
    return pl.pallas_call(
        kernel,
        out_shape=(
            jax.ShapeDtypeStruct((512, 512), BF),
            jax.ShapeDtypeStruct((64, 128), F32),
            jax.ShapeDtypeStruct((9, 64, 69), F32),
        ),
        in_specs=[any_] * 4,
        out_specs=(any_, inside, inside),
        scratch_shapes=scratch,
        compiler_params=pltpu.CompilerParams(vmem_limit_bytes=56 * 1024 * 1024, has_side_effects=True),
    )(t, wc, w, tg)


def body(fields, conv_weight, embed_weight, token_grads):
    t = jnp.pad(fields.transpose(1, 0, 2), ((0, 0), (0, CP - 69), (0, 0)))
    wc = jnp.pad(conv_weight.reshape(64, 3, 3, 69), ((0, 0), (0, 0), (0, 0), (0, CP - 69)))
    wc = jnp.pad(wc.reshape(64, 3, 3 * CP), ((0, 0), (0, 0), (0, 16))).transpose(1, 0, 2)
    embedded, embed_gradient, conv_gradient = step(t, wc, embed_weight, token_grads.reshape(512, 1024))
    return embedded.reshape(1, 1, 512, 512), conv_gradient.transpose(1, 0, 2), embed_gradient


def solution(mesh):
    return jax.shard_map(
        body,
        mesh=mesh,
        in_specs=(P(None, "lat", "lon"), P("ch", None, None), P(), P("lon", "lat", None, None)),
        out_specs=(P("lon", "lat", None, "ch"), P("ch", None, None), P("ch", ("lon", "lat"))),
        check_vma=False,
    )
```

```python
import functools

import jax
import jax.numpy as jnp
from jax import lax
from jax.experimental import pallas as pl
from jax.experimental.pallas import tpu as pltpu
from jax.sharding import PartitionSpec as P

BF = jnp.bfloat16
F32 = jnp.float32
MESH = pl.DeviceIdType.MESH
CP = 80
NN = (((1,), (0,)), ((), ()))
NT = (((1,), (1,)), ((), ()))


def dot(x, y, dims=NN):
    return lax.dot_general(x, y, dims, preferred_element_type=F32)


def one_hot(target, rows):
    index = lax.broadcasted_iota(jnp.int32, (rows, target.shape[1]), 0)
    return jnp.where(index == target, 1.0, 0.0).astype(BF)


def kernel(
    t_ref, wc_ref, w_ref, tg_ref,
    emb_out, eg_out, cg_out,
    slab, halo_l, halo_r, got_l, got_r, pack_l, pack_r,
    wc, wv, tgo, tgp, src, p1, xs, hid, hidp, hidt, dgelu, emb,
    egb, ego, ra, sbf, sbb, rb, scf, scb, rc,
    cga, cgp, scg, rcg, l0, rl, l1, agb, full,
    loc, tg_s, tg_r, ha_s, ha_r, pk_s, pk_r, wc_s, wc_r, em_s, em_r, tf_s, tf_r, hp_s, hp_r,
    a_s, a_r, b_s, b_r, c_s, c_r, q_s, q_r, d_s, d_r, e_s, e_r, f_s, f_r,
):
    lon = lax.axis_index("lon")
    lat = lax.axis_index("lat")
    ch = lax.axis_index("ch")
    hi = lon // 8
    lo = lax.rem(lon, 8)
    y = lat // 2
    xlo = lax.rem(lat, 2)
    other = 1 - ch

    def remote(source, target, send, recv, to_lon, to_lat, to_ch):
        return pltpu.make_async_remote_copy(
            src_ref=source, dst_ref=target, send_sem=send, recv_sem=recv,
            device_id=(to_lon, to_lat, to_ch), device_id_type=MESH,
        )

    barrier = pltpu.get_barrier_semaphore()

    def greet(to_lon, to_lat, to_ch):
        pl.semaphore_signal(barrier, inc=1, device_id=(to_lon, to_lat, to_ch), device_id_type=MESH)

    for i in range(1, 16):
        greet(lax.rem(lon + i, 16), lat, ch)
        greet(lax.rem(lon + i, 16), lat, other)
    greet(lon, lat, other)
    for i in range(1, 8):
        greet(lon, lax.rem(lat + i, 8), ch)

    @pl.when(lat > 0)
    def _():
        greet(lax.rem(lon + 1, 16), lat - 1, ch)
        greet(lax.rem(lon + 15, 16), lat - 1, ch)

    @pl.when(lat < 7)
    def _():
        greet(lax.rem(lon + 1, 16), lat + 1, ch)
        greet(lax.rem(lon + 15, 16), lat + 1, ch)

    slab_copy = pltpu.make_async_copy(t_ref.at[pl.ds(31 * ch, 33)], slab.at[pl.ds(other, 33)], loc.at[0])
    slab_copy.start()

    own_half = pl.ds(pl.multiple_of(64 * ch, 64), 64)
    for da in range(3):
        gap = jnp.zeros((64, CP - 69), F32)
        parts = []
        for db in range(3):
            parts += [wc_ref[3 * da + db].astype(F32), gap]
        wc[da, own_half] = jnp.concatenate(parts + [jnp.zeros((64, 16), F32)], axis=1).astype(BF)
    w_copies = [
        pltpu.make_async_copy(w_ref.at[:, pl.ds(1024 * s, 1024)], wv.at[s], loc.at[2 + s]) for s in range(16)
    ]
    for c in w_copies:
        c.start()

    j = lax.broadcasted_iota(jnp.int32, (1, 768), 1)
    column = 4 * (j % 32) + j // 128 - 1
    target = jnp.where((column >= 0) & (column < 128), column + 128 * ((j % 128) // 32), -1)
    p1[...] = one_hot(target, 512)
    xs[:, 480:496, :] = jnp.zeros((6, 16, 256), BF)
    cga[...] = jnp.zeros_like(cga)

    slab_copy.wait()
    lane = lax.broadcasted_iota(jnp.int32, (CP, 128), 1)
    left = jnp.zeros((CP, 128), F32)
    right = jnp.zeros((CP, 128), F32)
    for m in range(33):
        row = slab[other + m].astype(F32)
        if m:
            row = pltpu.roll(row, m, 1)
        left = jnp.where(lane == (m + 127) % 128, row, left)
        right = jnp.where(lane == m, row, right)
    pack_l[...] = left.astype(BF)
    pack_r[...] = right.astype(BF)
    @pl.when((lat == 0) | (lat == 7))
    def _():
        pl.semaphore_wait(barrier, 40)

    @pl.when((lat > 0) & (lat < 7))
    def _():
        pl.semaphore_wait(barrier, 42)

    def halo_copies(row, to_lat, base):
        out = []
        for n, (shift, target) in enumerate(((0, slab.at[33 * ch]), (1, halo_l), (15, halo_r))):
            to = lax.rem(base + shift, 16)
            out.append(remote(t_ref.at[row], target, ha_s.at[n], ha_r.at[n], to, to_lat, ch))
        return out

    inner = halo_copies(63 * other, lat + 1 - 2 * ch, lon)
    polar_s = []
    for n, (shift, target) in enumerate(((0, slab.at[33 * ch]), (1, halo_l), (15, halo_r))):
        to = lax.rem(lon + 8 + shift, 16)
        polar_s.append(remote(t_ref.at[63 * ch], target, ha_s.at[3 + n], ha_r.at[n], to, lat, ch))
    has_inner = lat != 7 * other
    has_polar = lat == 7 * ch

    @pl.when(has_inner)
    def _():
        for c in inner:
            c.start()

    @pl.when(has_polar)
    def _():
        for c in polar_s:
            c.start()

    pk0 = remote(pack_l, got_l, pk_s.at[0], pk_r.at[0], lax.rem(lon + 1, 16), lat, ch)
    pk1 = remote(pack_r, got_r, pk_s.at[1], pk_r.at[1], lax.rem(lon + 15, 16), lat, ch)
    pk0.start()
    pk1.start()

    wc_remote = remote(wc.at[:, own_half], wc.at[:, own_half], wc_s, wc_r, lon, lat, other)
    wc_remote.start()

    order = (2, 1, 3, 0)
    tg_copies = {}
    for n in order:
        columns = pl.ds(pl.multiple_of(256 * lax.rem(y + n, 4), 256), 256)
        for i in (4, 3, 5, 2, 6, 1, 7, 0):
            to = 8 * ch + lax.rem(lo + i, 8)
            rows = pl.ds(pl.multiple_of(32 * to, 32), 32)
            place = pl.ds(pl.multiple_of(32 * lo, 32), 32)
            c = remote(
                tg_ref.at[rows, columns], tgo.at[place, columns], tg_s.at[n, i], tg_r.at[n, i], to, lat, hi,
            )
            tg_copies[n, i] = c
            if i:
                c.start()
            else:

                @pl.when(ch == hi)
                def _():
                    pltpu.make_async_copy(tg_ref.at[rows, columns], tgo.at[place, columns], tg_r.at[n, 0]).start()

                @pl.when(ch != hi)
                def _():
                    c.start()

    for c in inner:
        c.wait_recv()

    def gather_rows(u, _):
        for half in range(2):
            for k in range(4):
                src[u, pl.ds(CP * half, CP), 128 * k : 128 * k + 128] = slab[16 * half + 4 * k + u]
        return 0

    lax.fori_loop(0, 6, gather_rows, 0)
    pk0.wait_recv()
    pk1.wait_recv()
    edges = jnp.concatenate([got_l[...], got_r[...], halo_l[...], halo_r[...]], axis=1)
    j2 = lax.broadcasted_iota(jnp.int32, (1, 256), 1)
    side = j2 // 128
    at_edge = (j2 % 32) == 31 * side

    def depth(u, _):
        res = dot(src[u], p1[...])
        for half in range(2):
            row = 16 * half + u + 4 * ((j2 % 128) // 32)
            m = row - other
            own = jnp.where(side == 0, (m + 127) % 128, 128 + m)
            want = jnp.where(row == 33 * ch, jnp.where(side == 0, 256 + 127, 384), own)
            fill = dot(edges, one_hot(jnp.where(at_edge, want, -1), 512))
            part = res[CP * half : CP * half + CP]
            lanes = slice(128 * half, 128 * half + 128)
            xs[u, 0:CP, lanes] = (part[:, 0:128] + fill[:, 0:128]).astype(BF)
            for v in range(1, 5):
                xs[u, CP * v : CP * v + CP, lanes] = part[:, 128 * v : 128 * v + 128].astype(BF)
            xs[u, CP * 5 : CP * 6, lanes] = (part[:, 640:768] + fill[:, 128:256]).astype(BF)
        return 0

    lax.fori_loop(0, 6, depth, 0)

    wc_remote.wait_recv()

    def conv(s, _):
        a = s // 4
        first = pl.multiple_of(CP * (s % 4), 16)
        v = jnp.zeros((128, 256), F32)
        for da in range(3):
            v = v + dot(wc[da], xs[a + da, pl.ds(first, 256), :])
        root = 0.7978845608028654
        square = v * v
        th = jnp.tanh(root * v * (1.0 + 0.044715 * square))
        half = 0.5 * (1.0 + th)
        slope = half + 0.5 * v * (1.0 - th * th) * (root * (1.0 + 3 * 0.044715 * square))
        h = (v * half).astype(BF)
        dgelu[s] = slope
        hid[s] = h.reshape(2, 64, 256)
        hidt[:, pl.ds(pl.multiple_of(128 * s, 128), 128)] = h.T
        return 0

    lax.fori_loop(0, 16, conv, 0)
    hp = remote(hid.at[:, other], hidp, hp_s, hp_r, lon, lat, other)
    hp.start()

    for c in w_copies:
        c.wait()

    def embed(n, _):
        columns = pl.ds(pl.multiple_of(256 * n, 256), 256)
        part = jnp.zeros((256, 256), F32)
        for s in range(16):
            part = part + dot(hidt[:, 128 * s : 128 * s + 128], wv[s, :, columns])
        emb[n // 2, :, pl.ds(pl.multiple_of(256 * (n % 2), 256), 256)] = part.astype(BF)
        return 0

    lax.fori_loop(0, 4, embed, 0)
    emb_copies = {}
    for i in (4, 3, 5, 2, 6, 1, 7, 0):
        r = lax.rem(lo + i, 8)
        for g in range(2):
            emb_copies[i, g] = remote(
                emb.at[g, pl.ds(pl.multiple_of(32 * r, 32), 32)],
                emb_out.at[pl.ds(pl.multiple_of(32 * lon, 32), 32)],
                em_s.at[2 * i + g], em_r.at[2 * i + hi], 8 * ch + r, lat, g,
            )
            if i:
                emb_copies[i, g].start()
            else:
                mine = (ch == hi) & (ch == g)

                @pl.when(mine)
                def _(g=g):
                    pltpu.make_async_copy(
                        emb.at[g, pl.ds(pl.multiple_of(32 * lo, 32), 32)],
                        emb_out.at[pl.ds(pl.multiple_of(32 * lon, 32), 32)],
                        em_r.at[hi],
                    ).start()

                @pl.when(jnp.logical_not(mine))
                def _(g=g):
                    emb_copies[0, g].start()

    def a_copy(cc, n):
        rows = pl.ds(pl.multiple_of(256 * cc, 256), 256)
        return remote(
            egb.at[n - 1, rows], ra.at[n - 1, rows], a_s.at[cc, n - 1], a_r.at[cc, n - 1],
            lon, lax.rem(lat + 2 * n, 8), ch,
        )

    def eg_part(cc, n):
        columns = pl.ds(pl.multiple_of(256 * lax.rem(y + n, 4), 256), 256)
        mine = hid[pl.ds(4 * cc, 4), ch].reshape(256, 256)
        theirs = hidp[pl.ds(4 * cc, 4)].reshape(256, 256)
        return dot(mine, tgo[:, columns]) + dot(theirs, tgp[:, columns])

    forwards = []
    for n in order:
        for i in range(8):
            tg_copies[n, i].wait_recv()
        columns = pl.ds(pl.multiple_of(256 * lax.rem(y + n, 4), 256), 256)
        c = remote(tgo.at[:, columns], tgp.at[:, columns], tf_s.at[n], tf_r.at[n], lon, lat, other)
        c.start()
        forwards.append(c)
        if n == 2:
            hp.wait_recv()
        c.wait_recv()

        def stage_a(cc, _, n=n):
            rows = pl.ds(pl.multiple_of(256 * cc, 256), 256)
            if n:
                egb[n - 1, rows] = eg_part(cc, n).astype(BF)
                a_copy(cc, n).start()
            else:
                ego[rows] = eg_part(cc, 0)
            return 0

        lax.fori_loop(0, 4, stage_a, 0)


    def conv_grad(a, _):
        hg = dot(wv[pl.ds(4 * a, 4)].reshape(512, 1024), tgo[...], NT)
        pg = (hg * dgelu[pl.ds(4 * a, 4)].reshape(512, 256)).astype(BF)
        for b in range(4):
            for da in range(3):
                cga[da] += dot(pg[128 * b : 128 * b + 128], xs[a + da, CP * b : CP * b + 256, :], NT)
        return 0

    lax.fori_loop(0, 4, conv_grad, 0)
    theirs = pl.ds(pl.multiple_of(64 * other, 64), 64)
    q_copy = remote(cga.at[:, theirs, :], cgp, q_s, q_r, lon, lat, other)
    q_copy.start()

    def b_copy(cc):
        rows = pl.ds(pl.multiple_of(256 * cc, 256), 256)
        return remote(sbb.at[other_x, rows], rb.at[rows], b_s.at[cc], b_r.at[cc], lon, lat + 1 - 2 * xlo, ch)

    other_x = 1 - xlo

    def stage_b(cc, _):
        rows = pl.ds(pl.multiple_of(256 * cc, 256), 256)
        total = ego[rows]
        for n in (1, 3, 2):
            a_copy(cc, n).wait_recv()
            total = total + ra[n - 1, rows].astype(F32)
        for g in range(2):
            piece = total[:, 128 * g : 128 * g + 128]
            sbf[g, rows] = piece
            sbb[g, rows] = piece.astype(BF)
        b_copy(cc).start()
        return 0

    def c_copy(s):
        i = lax.rem(s - lon + 16, 16)
        return remote(scb.at[s], rc.at[i], c_s.at[i], c_r.at[i], s, lat, ch)

    def stage_c(cc, _):
        rows = pl.ds(pl.multiple_of(256 * cc, 256), 256)
        b_copy(cc).wait_recv()
        total = (sbf[xlo, rows] + rb[rows].astype(F32)).reshape(4, 64, 128)
        scf[pl.ds(4 * cc, 4)] = total
        scb[pl.ds(4 * cc, 4)] = total.astype(BF)
        for k in range(4):
            s = 4 * cc + k

            @pl.when(s != lon)
            def _():
                c_copy(s).start()

        return 0

    def d_copy(i):
        to = lax.rem(lon + i, 16)
        return remote(scg.at[to], rcg.at[i], d_s.at[i], d_r.at[i], to, lat, ch)

    def e_copy(i):
        return remote(l0, rl.at[lat], e_s.at[i], e_r.at[i], lon, lax.rem(lat + i, 8), ch)

    def f_copy(i):
        return remote(l1, agb.at[lon], f_s.at[i], f_r.at[i], lax.rem(lon + i, 16), lat, ch)

    q_copy.wait_recv()
    total = cga[:, pl.ds(pl.multiple_of(64 * ch, 64), 64), :] + cgp[...]
    for n in range(16):
        ob, half = n // 2, n % 2
        scg[n] = total[:, 8 * ob : 8 * ob + 8, 128 * half : 128 * half + 128]
    for i in range(1, 16):
        d_copy(i).start()

    stage_b(0, 0)

    total = scg[lon]
    for i in range(1, 16):
        d_copy(i).wait_recv()
        total = total + rcg[i]
    l0[...] = total
    rl[lat] = total
    for i in range(1, 8):
        e_copy(i).start()

    stage_b(1, 0)
    stage_c(0, 0)

    for i in range(1, 8):
        e_copy(i).wait_recv()
    total = rl[0]
    for i in range(1, 8):
        total = total + rl[i]
    l1[...] = total
    agb[lon] = total
    for i in range(1, 16):
        f_copy(i).start()

    stage_b(2, 0)
    stage_c(1, 0)
    stage_b(3, 0)
    stage_c(2, 0)

    for i in range(1, 16):
        f_copy(i).wait_recv()
    for n in range(16):
        ob, half = n // 2, n % 2
        full[:, 8 * ob : 8 * ob + 8, 128 * half : 128 * half + 128] = agb[n]
    for da in range(3):
        for db in range(3):
            cg_out[3 * da + db] = full[da, :, CP * db : CP * db + 69]

    stage_c(3, 0)
    total = scf[lon]
    for i in range(1, 16):
        remote(scb.at[0], rc.at[i], c_s.at[i], c_r.at[i], lon, lat, other).wait_recv()
        total = total + rc[i].astype(F32)
    eg_out[...] = total

    for i in range(8):
        for g in range(2):
            remote(
                emb.at[0, pl.ds(0, 32)], emb_out.at[pl.ds(0, 32)],
                em_s.at[0], em_r.at[2 * i + g], lon, lat, other,
            ).wait_recv()

    @pl.when(has_inner)
    def _():
        for c in inner:
            c.wait_send()

    @pl.when(has_polar)
    def _():
        for c in polar_s:
            c.wait_send()

    wc_remote.wait_send()
    for n in order:
        for i in range(1, 8):
            tg_copies[n, i].wait_send()

    @pl.when(ch != hi)
    def _():
        for n in order:
            tg_copies[n, 0].wait_send()

    pk0.wait_send()
    pk1.wait_send()
    hp.wait_send()
    q_copy.wait_send()
    for c in forwards:
        c.wait_send()
    for (i, g), c in emb_copies.items():
        if i:
            c.wait_send()
        else:

            @pl.when(jnp.logical_not((ch == hi) & (ch == g)))
            def _(c=c):
                c.wait_send()

    for cc in range(4):
        for n in (1, 2, 3):
            a_copy(cc, n).wait_send()
        b_copy(cc).wait_send()
    for i in range(1, 16):
        remote(scb.at[0], rc.at[i], c_s.at[i], c_r.at[i], lon, lat, other).wait_send()
        d_copy(i).wait_send()
        f_copy(i).wait_send()
    for i in range(1, 8):
        e_copy(i).wait_send()


def step(t, wc, w, tg):
    vm = pltpu.VMEM
    sem = pltpu.SemaphoreType.DMA
    scratch = [
        vm((34, CP, 128), BF), vm((CP, 128), BF), vm((CP, 128), BF), vm((CP, 128), BF), vm((CP, 128), BF),
        vm((CP, 128), BF), vm((CP, 128), BF),
        vm((3, 128, 256), BF), vm((16, 128, 1024), BF), vm((256, 1024), BF), vm((256, 1024), BF),
        vm((6, 2 * CP, 512), BF), vm((512, 768), BF), vm((6, 496, 256), BF),
        vm((16, 2, 64, 256), BF), vm((16, 64, 256), BF), vm((256, 2048), BF), vm((16, 128, 256), F32),
        vm((2, 256, 512), BF),
        vm((3, 1024, 256), BF), vm((1024, 256), F32), vm((3, 1024, 256), BF),
        vm((2, 1024, 128), F32), vm((2, 1024, 128), BF), vm((1024, 128), BF),
        vm((16, 64, 128), F32), vm((16, 64, 128), BF), vm((16, 64, 128), BF),
        vm((3, 128, 256), F32), vm((3, 64, 256), F32), vm((16, 3, 8, 128), F32), vm((16, 3, 8, 128), F32),
        vm((3, 8, 128), F32), vm((8, 3, 8, 128), F32), vm((3, 8, 128), F32), vm((16, 3, 8, 128), F32),
        vm((3, 64, 256), F32),
        sem((18,)), sem((4, 8)), sem((4, 8)), sem((6,)), sem((3,)), sem((2,)), sem((2,)), sem, sem,
        sem((16,)), sem((16,)), sem((4,)), sem((4,)), sem, sem,
        sem((4, 3)), sem((4, 3)), sem((4,)), sem((4,)), sem((16,)), sem((16,)), sem, sem,
        sem((16,)), sem((16,)), sem((8,)), sem((8,)), sem((16,)), sem((16,)),
    ]
    any_ = pl.BlockSpec(memory_space=pl.ANY)
    inside = pl.BlockSpec(memory_space=pltpu.VMEM)
    return pl.pallas_call(
        kernel,
        out_shape=(
            jax.ShapeDtypeStruct((512, 512), BF),
            jax.ShapeDtypeStruct((64, 128), F32),
            jax.ShapeDtypeStruct((9, 64, 69), F32),
        ),
        in_specs=[any_, inside, any_, any_],
        out_specs=(any_, inside, inside),
        scratch_shapes=scratch,
        compiler_params=pltpu.CompilerParams(vmem_limit_bytes=56 * 1024 * 1024, has_side_effects=True, collective_id=0),
    )(t, wc, w, tg)


def settle(emb, eg, cg, emb_out, eg_out, cg_out):
    emb_out[...] = emb[...]

    @pl.when(pl.program_id(0) == 0)
    def _():
        eg_out[...] = eg[...]
        cg_out[...] = cg[...]


def body(fields, conv_weight, embed_weight, token_grads):
    t = jnp.pad(fields.transpose(1, 0, 2), ((0, 0), (0, CP - 69), (0, 0)))
    embedded, embed_gradient, conv_gradient = step(t, conv_weight.transpose(1, 0, 2), embed_weight, token_grads.reshape(512, 1024))
    specs = [
        pl.BlockSpec((128, 512), lambda n: (n, 0)),
        pl.BlockSpec((64, 128), lambda n: (0, 0)),
        pl.BlockSpec((9, 64, 69), lambda n: (0, 0, 0)),
    ]
    embedded, embed_gradient, conv_gradient = pl.pallas_call(
        settle,
        grid=(4,),
        out_shape=tuple(jax.ShapeDtypeStruct(a.shape, a.dtype) for a in (embedded, embed_gradient, conv_gradient)),
        in_specs=specs,
        out_specs=tuple(specs),
    )(embedded, embed_gradient, conv_gradient)
    return embedded.reshape(1, 1, 512, 512), conv_gradient.transpose(1, 0, 2), embed_gradient


def solution(mesh):
    return jax.shard_map(
        body,
        mesh=mesh,
        in_specs=(P(None, "lat", "lon"), P("ch", None, None), P(), P("lon", "lat", None, None)),
        out_specs=(P("lon", "lat", None, "ch"), P("ch", None, None), P("ch", ("lon", "lat"))),
        check_vma=False,
    )
```

```python
import functools

import jax
import jax.numpy as jnp
from jax import lax
from jax.experimental import pallas as pl
from jax.experimental.pallas import tpu as pltpu
from jax.sharding import PartitionSpec as P

BF = jnp.bfloat16
F32 = jnp.float32
MESH = pl.DeviceIdType.MESH
CP = 80
NN = (((1,), (0,)), ((), ()))
NT = (((1,), (1,)), ((), ()))


def dot(x, y, dims=NN):
    return lax.dot_general(x, y, dims, preferred_element_type=F32)


def one_hot(target, rows):
    index = lax.broadcasted_iota(jnp.int32, (rows, target.shape[1]), 0)
    return jnp.where(index == target, 1.0, 0.0).astype(BF)


def kernel(
    t_ref, wc_ref, w_ref, tg_ref,
    emb_out, eg_out, cg_out,
    narrow, wide, edge, slab, halo_l, halo_r, got_l, got_r, pack_l, pack_r,
    wc, wv, tgo, tgp, src, p1, xs, hid, hidp, hidt, dgelu, emb,
    ysb, yrb, yown, yxs, yxr, ycf, xsb, xrb, xown, xys, xyr, xcf, scf, scb, rc,
    cga, cgp, scg, scb16, rcg, l0, rl, l1, agb, full,
    loc, tg_s, tg_r, ha_s, ha_r, pk_s, pk_r, wc_s, wc_r, em_s, em_r, tf_s, tf_r, hp_s, hp_r,
    ya_s, ya_r, yb_s, yb_r, xa_s, xa_r, xb_s, xb_r, c_s, c_r, q_s, q_r, d_s, d_r, e_s, e_r, f_s, f_r,
):
    lon = lax.axis_index("lon")
    lat = lax.axis_index("lat")
    ch = lax.axis_index("ch")
    hi = lon // 8
    lo = lax.rem(lon, 8)
    y = lat // 2
    xlo = lax.rem(lat, 2)
    other = 1 - ch

    def remote(source, target, send, recv, to_lon, to_lat, to_ch):
        return pltpu.make_async_remote_copy(
            src_ref=source, dst_ref=target, send_sem=send, recv_sem=recv,
            device_id=(to_lon, to_lat, to_ch), device_id_type=MESH,
        )

    barrier = pltpu.get_barrier_semaphore()

    def greet(to_lon, to_lat, to_ch):
        pl.semaphore_signal(barrier, inc=1, device_id=(to_lon, to_lat, to_ch), device_id_type=MESH)

    for i in range(1, 16):
        greet(lax.rem(lon + i, 16), lat, ch)
        greet(lax.rem(lon + i, 16), lat, other)
    greet(lon, lat, other)
    for i in range(1, 8):
        greet(lon, lax.rem(lat + i, 8), ch)

    @pl.when(lat > 0)
    def _():
        greet(lax.rem(lon + 1, 16), lat - 1, ch)
        greet(lax.rem(lon + 15, 16), lat - 1, ch)

    @pl.when(lat < 7)
    def _():
        greet(lax.rem(lon + 1, 16), lat + 1, ch)
        greet(lax.rem(lon + 15, 16), lat + 1, ch)

    field_copy = pltpu.make_async_copy(t_ref, narrow, loc.at[0])
    field_copy.start()

    own_half = pl.ds(pl.multiple_of(64 * ch, 64), 64)
    for da in range(3):
        gap = jnp.zeros((64, CP - 69), F32)
        parts = []
        for db in range(3):
            parts += [wc_ref[3 * da + db].astype(F32), gap]
        wc[da, own_half] = jnp.concatenate(parts + [jnp.zeros((64, 16), F32)], axis=1).astype(BF)
    w_copies = [
        pltpu.make_async_copy(w_ref.at[:, pl.ds(1024 * s, 1024)], wv.at[s], loc.at[2 + s]) for s in range(16)
    ]
    for c in w_copies:
        c.start()

    j = lax.broadcasted_iota(jnp.int32, (1, 768), 1)
    column = 4 * (j % 32) + j // 128 - 1
    target = jnp.where((column >= 0) & (column < 128), column + 128 * ((j % 128) // 32), -1)
    p1[...] = one_hot(target, 512)
    xs[:, 480:496, :] = jnp.zeros((6, 16, 256), BF)
    cga[...] = jnp.zeros_like(cga)

    wide[4416:5120] = jnp.zeros((704, 128), F32)
    field_copy.wait()

    def widen(c, _):
        wide[pl.ds(pl.multiple_of(64 * c, 64), 64)] = narrow[c].astype(F32)
        return 0

    lax.fori_loop(0, 69, widen, 0, unroll=3)
    edge[...] = wide[pl.ds(63 * other, CP, stride=64)].astype(BF)
    lane = lax.broadcasted_iota(jnp.int32, (CP, 128), 1)
    left = jnp.zeros((CP, 128), F32)
    right = jnp.zeros((CP, 128), F32)
    for m in range(33):
        row = wide[pl.ds(31 * ch + m, CP, stride=64)]
        slab[other + m] = row.astype(BF)
        if m:
            row = pltpu.roll(row, m, 1)
        left = jnp.where(lane == (m + 127) % 128, row, left)
        right = jnp.where(lane == m, row, right)
    pack_l[...] = left.astype(BF)
    pack_r[...] = right.astype(BF)
    @pl.when((lat == 0) | (lat == 7))
    def _():
        pl.semaphore_wait(barrier, 40)

    @pl.when((lat > 0) & (lat < 7))
    def _():
        pl.semaphore_wait(barrier, 42)

    def halo_copies(to_lat, base):
        out = []
        for n, (shift, target) in enumerate(((0, slab.at[33 * ch]), (1, halo_l), (15, halo_r))):
            to = lax.rem(base + shift, 16)
            out.append(remote(edge, target, ha_s.at[n], ha_r.at[n], to, to_lat, ch))
        return out

    inner = halo_copies(lat + 1 - 2 * ch, lon)
    polar_s = []
    for n, (shift, target) in enumerate(((0, slab.at[33 * ch]), (1, halo_l), (15, halo_r))):
        to = lax.rem(lon + 8 + shift, 16)
        polar_s.append(remote(slab.at[1 + 31 * ch], target, ha_s.at[3 + n], ha_r.at[n], to, lat, ch))
    has_inner = lat != 7 * other
    has_polar = lat == 7 * ch

    @pl.when(has_inner)
    def _():
        for c in inner:
            c.start()

    @pl.when(has_polar)
    def _():
        for c in polar_s:
            c.start()

    pk0 = remote(pack_l, got_l, pk_s.at[0], pk_r.at[0], lax.rem(lon + 1, 16), lat, ch)
    pk1 = remote(pack_r, got_r, pk_s.at[1], pk_r.at[1], lax.rem(lon + 15, 16), lat, ch)
    pk0.start()
    pk1.start()

    wc_remote = remote(wc.at[:, own_half], wc.at[:, own_half], wc_s, wc_r, lon, lat, other)
    wc_remote.start()

    order = (2, 1, 3, 0)
    tg_copies = {}
    for n in order:
        columns = pl.ds(pl.multiple_of(256 * lax.rem(y + n, 4), 256), 256)
        for i in (4, 3, 5, 2, 6, 1, 7, 0):
            to = 8 * ch + lax.rem(lo + i, 8)
            rows = pl.ds(pl.multiple_of(32 * to, 32), 32)
            place = pl.ds(pl.multiple_of(32 * lo, 32), 32)
            c = remote(
                tg_ref.at[rows, columns], tgo.at[place, columns], tg_s.at[n, i], tg_r.at[n, i], to, lat, hi,
            )
            tg_copies[n, i] = c
            if i:
                c.start()
            else:

                @pl.when(ch == hi)
                def _():
                    pltpu.make_async_copy(tg_ref.at[rows, columns], tgo.at[place, columns], tg_r.at[n, 0]).start()

                @pl.when(ch != hi)
                def _():
                    c.start()

    for c in inner:
        c.wait_recv()

    def gather_rows(u, _):
        for half in range(2):
            for k in range(4):
                src[u, pl.ds(CP * half, CP), 128 * k : 128 * k + 128] = slab[16 * half + 4 * k + u]
        return 0

    lax.fori_loop(0, 6, gather_rows, 0)
    pk0.wait_recv()
    pk1.wait_recv()
    edges = jnp.concatenate([got_l[...], got_r[...], halo_l[...], halo_r[...]], axis=1)
    j2 = lax.broadcasted_iota(jnp.int32, (1, 256), 1)
    side = j2 // 128
    at_edge = (j2 % 32) == 31 * side

    def depth(u, _):
        res = dot(src[u], p1[...])
        for half in range(2):
            row = 16 * half + u + 4 * ((j2 % 128) // 32)
            m = row - other
            own = jnp.where(side == 0, (m + 127) % 128, 128 + m)
            want = jnp.where(row == 33 * ch, jnp.where(side == 0, 256 + 127, 384), own)
            fill = dot(edges, one_hot(jnp.where(at_edge, want, -1), 512))
            part = res[CP * half : CP * half + CP]
            lanes = slice(128 * half, 128 * half + 128)
            xs[u, 0:CP, lanes] = (part[:, 0:128] + fill[:, 0:128]).astype(BF)
            for v in range(1, 5):
                xs[u, CP * v : CP * v + CP, lanes] = part[:, 128 * v : 128 * v + 128].astype(BF)
            xs[u, CP * 5 : CP * 6, lanes] = (part[:, 640:768] + fill[:, 128:256]).astype(BF)
        return 0

    lax.fori_loop(0, 6, depth, 0)

    wc_remote.wait_recv()

    def conv(s, _):
        a = s // 4
        first = pl.multiple_of(CP * (s % 4), 16)
        v = jnp.zeros((128, 256), F32)
        for da in range(3):
            v = v + dot(wc[da], xs[a + da, pl.ds(first, 256), :])
        root = 0.7978845608028654
        square = v * v
        th = jnp.tanh(root * v * (1.0 + 0.044715 * square))
        half = 0.5 * (1.0 + th)
        slope = half + 0.5 * v * (1.0 - th * th) * (root * (1.0 + 3 * 0.044715 * square))
        h = (v * half).astype(BF)
        dgelu[s] = slope
        hid[s] = h.reshape(2, 64, 256)
        hidt[:, pl.ds(pl.multiple_of(128 * s, 128), 128)] = h.T
        return 0

    lax.fori_loop(0, 16, conv, 0, unroll=2)
    hp = remote(hid.at[:, other], hidp, hp_s, hp_r, lon, lat, other)
    hp.start()
    for c in w_copies:
        c.wait()

    def embed(n, _):
        columns = pl.ds(pl.multiple_of(256 * n, 256), 256)
        part = jnp.zeros((256, 256), F32)
        for s in range(16):
            part = part + dot(hidt[:, 128 * s : 128 * s + 128], wv[s, :, columns])
        emb[n // 2, :, pl.ds(pl.multiple_of(256 * (n % 2), 256), 256)] = part.astype(BF)
        return 0

    lax.fori_loop(0, 4, embed, 0)
    emb_copies = {}
    for i in (4, 3, 5, 2, 6, 1, 7, 0):
        r = lax.rem(lo + i, 8)
        for g in range(2):
            emb_copies[i, g] = remote(
                emb.at[g, pl.ds(pl.multiple_of(32 * r, 32), 32)],
                emb_out.at[pl.ds(pl.multiple_of(32 * lon, 32), 32)],
                em_s.at[2 * i + g], em_r.at[2 * i + hi], 8 * ch + r, lat, g,
            )
            if i:
                emb_copies[i, g].start()
            else:
                mine = (ch == hi) & (ch == g)

                @pl.when(mine)
                def _(g=g):
                    pltpu.make_async_copy(
                        emb.at[g, pl.ds(pl.multiple_of(32 * lo, 32), 32)],
                        emb_out.at[pl.ds(pl.multiple_of(32 * lon, 32), 32)],
                        em_r.at[hi],
                    ).start()

                @pl.when(jnp.logical_not(mine))
                def _(g=g):
                    emb_copies[0, g].start()

    def ya_copy(n):
        return remote(
            ysb.at[n - 1], yrb.at[n - 1], ya_s.at[n - 1], ya_r.at[n - 1], lon, lax.rem(lat + 2 * n, 8), ch
        )

    def yb_copy():
        return remote(yxs, yxr, yb_s, yb_r, lon, lat + 1 - 2 * xlo, ch)

    def xa_copy(n):
        return remote(xsb.at[n], xrb.at[n], xa_s.at[n], xa_r.at[n], lon, lat + 1 - 2 * xlo, ch)

    def xb_copy(n):
        return remote(
            xys.at[n - 1], xyr.at[n - 1], xb_s.at[n - 1], xb_r.at[n - 1], lon, lax.rem(lat + 2 * n, 8), ch
        )

    def split(value):
        first, second = value[:, 0:128], value[:, 128:256]
        return jnp.where(xlo == 0, first, second), jnp.where(xlo == 0, second, first)

    def block(n):
        return pl.ds(pl.multiple_of(256 * lax.rem(y + n, 4), 256), 256)

    def embed_part(n):
        def some(c, _):
            mine = hid[pl.ds(4 * c, 4), ch].reshape(256, 256)
            theirs = hidp[pl.ds(4 * c, 4)].reshape(256, 256)
            part = dot(mine, tgo[:, block(n)]) + dot(theirs, tgp[:, block(n)])

            @pl.when(c < 2)
            def _():
                rows = pl.ds(pl.multiple_of(256 * c, 256), 256)
                if n:
                    ysb[n - 1, rows] = part.astype(BF)
                else:
                    yown[rows] = part

            @pl.when(c >= 2)
            def _():
                rows = pl.ds(pl.multiple_of(256 * (c - 2), 256), 256)
                near, far = split(part)
                xown[n, rows] = near
                xsb[n, rows] = far.astype(BF)

            return 0

        lax.fori_loop(0, 4, some, 0)
        xa_copy(n).start()
        if n:
            ya_copy(n).start()

    def stage_xb(n):
        xa_copy(n).wait_recv()
        total = xown[n] + xrb[n].astype(F32)
        if n:
            xys[n - 1] = total.astype(BF)
            xb_copy(n).start()
        else:
            xcf[...] = total

    forwards = {}
    last = None
    for n in order:
        for i in range(8):
            tg_copies[n, i].wait_recv()
        forwards[n] = remote(tgo.at[:, block(n)], tgp.at[:, block(n)], tf_s.at[n], tf_r.at[n], lon, lat, other)
        forwards[n].start()
        if last is None:
            hp.wait_recv()
        else:
            forwards[last].wait_recv()
            embed_part(last)
        last = n

    def conv_grad(a, _):
        hg = dot(wv[pl.ds(4 * a, 4)].reshape(512, 1024), tgo[...], NT)
        pg = (hg * dgelu[pl.ds(4 * a, 4)].reshape(512, 256)).astype(BF)
        for da in range(3):
            total = cga[da]
            for b in range(4):
                total = total + dot(pg[128 * b : 128 * b + 128], xs[a + da, CP * b : CP * b + 256, :], NT)
            cga[da] = total
        return 0

    lax.fori_loop(0, 4, conv_grad, 0, unroll=2)
    half_o = pl.ds(pl.multiple_of(64 * other, 64), 64)
    q_copy = remote(cga.at[:, half_o, :], cgp, q_s, q_r, lon, lat, other)
    q_copy.start()
    forwards[0].wait_recv()
    embed_part(0)
    stage_xb(2)
    stage_xb(1)

    def d_copy(j):
        i = lax.rem(j - lon + 16, 16)
        return remote(scb16.at[j], rcg.at[i], d_s.at[j], d_r.at[i], j, lat, ch)

    def e_copy(i):
        return remote(l0, rl.at[lat], e_s.at[i], e_r.at[i], lon, lax.rem(lat + i, 8), ch)

    def f_copy(i):
        return remote(l1, agb.at[lon], f_s.at[i], f_r.at[lon], lax.rem(lon + i, 16), lat, ch)

    q_copy.wait_recv()
    total = cga[:, pl.ds(pl.multiple_of(64 * ch, 64), 64), :] + cgp[...]
    for j in range(12):
        for half in range(2):
            piece = total[j // 4, 16 * (j % 4) : 16 * (j % 4) + 16, 128 * half : 128 * half + 128]
            scg[j, half] = piece
            scb16[j, half] = piece.astype(BF)
    for j in range(12):

        @pl.when(j != lon)
        def _(j=j):
            d_copy(j).start()

    stage_xb(3)
    stage_xb(0)

    total = yown[...]
    for n in (1, 3, 2):
        ya_copy(n).wait_recv()
        total = total + yrb[n - 1].astype(F32)
    near, far = split(total)
    ycf[...] = near
    yxs[...] = far.astype(BF)
    yb_copy().start()

    @pl.when(lon < 12)
    def _():
        total = scg[lon]
        for i in range(1, 16):
            remote(scb16.at[0], rcg.at[i], d_s.at[0], d_r.at[i], lon, lat, other).wait_recv()
            total = total + rcg[i].astype(F32)
        l0[...] = total
        rl[lat] = total
        for i in range(1, 8):
            e_copy(i).start()

    def c_copy(s):
        i = lax.rem(s - lon + 16, 16)
        return remote(scb.at[s], rc.at[i], c_s.at[i], c_r.at[i], s, lat, ch)

    def stage_c(first, total):
        total = total.reshape(8, 64, 128)
        scf[first : first + 8] = total
        scb[first : first + 8] = total.astype(BF)
        for s in range(first, first + 8):

            @pl.when(s != lon)
            def _(s=s):
                c_copy(s).start()

    total = xcf[...]
    for n in (1, 3, 2):
        xb_copy(n).wait_recv()
        total = total + xyr[n - 1].astype(F32)
    stage_c(8, total)
    yb_copy().wait_recv()
    stage_c(0, ycf[...] + yxr[...].astype(F32))

    @pl.when(lon < 12)
    def _():
        for i in range(1, 8):
            e_copy(i).wait_recv()
        total = rl[0]
        for i in range(1, 8):
            total = total + rl[i]
        total = total.astype(BF)
        l1[...] = total
        agb[lon] = total
        for i in range(1, 16):
            f_copy(i).start()

    total = scf[lon]
    for i in range(1, 16):
        remote(scb.at[0], rc.at[i], c_s.at[i], c_r.at[i], lon, lat, other).wait_recv()
        total = total + rc[i].astype(F32)
    eg_out[...] = total

    for j in range(12):

        @pl.when(j != lon)
        def _(j=j):
            remote(l1, agb.at[j], f_s.at[0], f_r.at[j], lon, lat, other).wait_recv()

        for half in range(2):
            full[j // 4, 16 * (j % 4) : 16 * (j % 4) + 16, 128 * half : 128 * half + 128] = agb[j, half].astype(F32)
    for da in range(3):
        for db in range(3):
            cg_out[3 * da + db] = full[da, :, CP * db : CP * db + 69]

    for i in range(8):
        for g in range(2):
            remote(
                emb.at[0, pl.ds(0, 32)], emb_out.at[pl.ds(0, 32)],
                em_s.at[0], em_r.at[2 * i + g], lon, lat, other,
            ).wait_recv()

    @pl.when(has_inner)
    def _():
        for c in inner:
            c.wait_send()

    @pl.when(has_polar)
    def _():
        for c in polar_s:
            c.wait_send()

    wc_remote.wait_send()
    for n in order:
        for i in range(1, 8):
            tg_copies[n, i].wait_send()

    @pl.when(ch != hi)
    def _():
        for n in order:
            tg_copies[n, 0].wait_send()

    pk0.wait_send()
    pk1.wait_send()
    hp.wait_send()
    q_copy.wait_send()
    for c in forwards.values():
        c.wait_send()
    for (i, g), c in emb_copies.items():
        if i:
            c.wait_send()
        else:

            @pl.when(jnp.logical_not((ch == hi) & (ch == g)))
            def _(c=c):
                c.wait_send()

    for n in (1, 2, 3):
        ya_copy(n).wait_send()
        xb_copy(n).wait_send()
    yb_copy().wait_send()
    for n in range(4):
        xa_copy(n).wait_send()
    for i in range(1, 16):
        remote(scb.at[0], rc.at[i], c_s.at[i], c_r.at[i], lon, lat, other).wait_send()
    for j in range(12):

        @pl.when(j != lon)
        def _(j=j):
            d_copy(j).wait_send()

    @pl.when(lon < 12)
    def _():
        for i in range(1, 16):
            f_copy(i).wait_send()
        for i in range(1, 8):
            e_copy(i).wait_send()


def step(t, wc, w, tg):
    vm = pltpu.VMEM
    sem = pltpu.SemaphoreType.DMA
    scratch = [
        vm((69, 64, 128), BF), vm((64 * CP, 128), F32), vm((CP, 128), BF), vm((34, CP, 128), BF), vm((CP, 128), BF), vm((CP, 128), BF), vm((CP, 128), BF), vm((CP, 128), BF),
        vm((CP, 128), BF), vm((CP, 128), BF),
        vm((3, 128, 256), BF), vm((16, 128, 1024), BF), vm((256, 1024), BF), vm((256, 1024), BF),
        vm((6, 2 * CP, 512), BF), vm((512, 768), BF), vm((6, 496, 256), BF),
        vm((16, 2, 64, 256), BF), vm((16, 64, 256), BF), vm((256, 2048), BF), vm((16, 128, 256), F32),
        vm((2, 256, 512), BF),
        vm((3, 512, 256), BF), vm((3, 512, 256), BF), vm((512, 256), F32),
        vm((512, 128), BF), vm((512, 128), BF), vm((512, 128), F32),
        vm((4, 512, 128), BF), vm((4, 512, 128), BF), vm((4, 512, 128), F32),
        vm((3, 512, 128), BF), vm((3, 512, 128), BF), vm((512, 128), F32),
        vm((16, 64, 128), F32), vm((16, 64, 128), BF), vm((16, 64, 128), BF),
        vm((3, 128, 256), F32), vm((3, 64, 256), F32), vm((12, 2, 16, 128), F32), vm((12, 2, 16, 128), BF),
        vm((16, 2, 16, 128), BF), vm((2, 16, 128), F32), vm((8, 2, 16, 128), F32), vm((2, 16, 128), BF),
        vm((12, 2, 16, 128), BF), vm((3, 64, 256), F32),
        sem((18,)), sem((4, 8)), sem((4, 8)), sem((6,)), sem((3,)), sem((2,)), sem((2,)), sem, sem,
        sem((16,)), sem((16,)), sem((4,)), sem((4,)), sem, sem,
        sem((3,)), sem((3,)), sem, sem, sem((4,)), sem((4,)), sem((3,)), sem((3,)), sem((16,)), sem((16,)), sem, sem,
        sem((12,)), sem((16,)), sem((8,)), sem((8,)), sem((16,)), sem((12,)),
    ]
    any_ = pl.BlockSpec(memory_space=pl.ANY)
    inside = pl.BlockSpec(memory_space=pltpu.VMEM)
    return pl.pallas_call(
        kernel,
        out_shape=(
            jax.ShapeDtypeStruct((512, 512), BF),
            jax.ShapeDtypeStruct((64, 128), F32),
            jax.ShapeDtypeStruct((9, 64, 69), F32),
        ),
        in_specs=[any_, inside, any_, any_],
        out_specs=(any_, inside, inside),
        scratch_shapes=scratch,
        compiler_params=pltpu.CompilerParams(vmem_limit_bytes=56 * 1024 * 1024, has_side_effects=True, collective_id=0),
    )(t, wc, w, tg)


def settle(emb, eg, cg, emb_out, eg_out, cg_out, emb_held, eg_held, cg_held, sem):
    moves = []
    for n in range(4):
        rows = pl.ds(128 * n, 128)
        moves.append((emb.at[rows], emb_held.at[rows], emb_out.at[rows]))
    moves += [(eg, eg_held, eg_out), (cg, cg_held, cg_out)]
    moves = [
        (pltpu.make_async_copy(a, b, sem.at[0, n]), pltpu.make_async_copy(b, c, sem.at[1, n]))
        for n, (a, b, c) in enumerate(moves)
    ]
    for first, _ in moves:
        first.start()
    for first, second in moves:
        first.wait()
        second.start()
    for _, second in moves:
        second.wait()


def body(fields, conv_weight, embed_weight, token_grads):
    embedded, embed_gradient, conv_gradient = step(fields, conv_weight.transpose(1, 0, 2), embed_weight, token_grads.reshape(512, 1024))
    shapes = [(a.shape, a.dtype) for a in (embedded, embed_gradient, conv_gradient)]
    outside = pl.BlockSpec(memory_space=pltpu.HBM)
    embedded, embed_gradient, conv_gradient = pl.pallas_call(
        settle,
        out_shape=tuple(jax.ShapeDtypeStruct(*a) for a in shapes),
        in_specs=[outside] * 3,
        out_specs=(outside,) * 3,
        scratch_shapes=[pltpu.VMEM(*a) for a in shapes] + [pltpu.SemaphoreType.DMA((2, 6))],
    )(embedded, embed_gradient, conv_gradient)
    return embedded.reshape(1, 1, 512, 512), conv_gradient.transpose(1, 0, 2), embed_gradient


def solution(mesh):
    return jax.shard_map(
        body,
        mesh=mesh,
        in_specs=(P(None, "lat", "lon"), P("ch", None, None), P(), P("lon", "lat", None, None)),
        out_specs=(P("lon", "lat", None, "ch"), P("ch", None, None), P("ch", ("lon", "lat"))),
        check_vma=False,
    )
```

```python
import functools

import jax
import jax.numpy as jnp
from jax import lax
from jax.experimental import pallas as pl
from jax.experimental.pallas import tpu as pltpu
from jax.sharding import PartitionSpec as P

BF = jnp.bfloat16
F32 = jnp.float32
MESH = pl.DeviceIdType.MESH
CP = 80
NN = (((1,), (0,)), ((), ()))
NT = (((1,), (1,)), ((), ()))


def dot(x, y, dims=NN):
    return lax.dot_general(x, y, dims, preferred_element_type=F32)


def one_hot(target, rows):
    index = lax.broadcasted_iota(jnp.int32, (rows, target.shape[1]), 0)
    return jnp.where(index == target, 1.0, 0.0).astype(BF)


def kernel(
    t_ref, wc_ref, w_ref, tg_ref,
    emb_out, eg_out, cg_out,
    narrow, wide, edge, slab, halo_l, halo_r, got_l, got_r, pack_l, pack_r,
    wc, wv, tgo, tgp, src, p1, xs, hid, hidp, hidt, dgelu, emb,
    ysb, yrb, yown, yxs, yxr, ycf, xsb, xrb, xown, xys, xyr, xcf, scf, scb, rc,
    cga, cgp, scg, scb16, rcg, l0, rl, l1, agb, full,
    loc, tg_s, tg_r, ha_s, ha_r, pk_s, pk_r, wc_s, wc_r, em_s, em_r, tf_s, tf_r, hp_s, hp_r,
    a_s, a_r, b_s, b_r, xa_s, xa_r, xb_s, xb_r, c_s, c_r, q_s, q_r, d_s, d_r, e_s, e_r, f_s, f_r,
):
    lon = lax.axis_index("lon")
    lat = lax.axis_index("lat")
    ch = lax.axis_index("ch")
    hi = lon // 8
    lo = lax.rem(lon, 8)
    y = lat // 2
    xlo = lax.rem(lat, 2)
    other = 1 - ch

    def remote(source, target, send, recv, to_lon, to_lat, to_ch):
        return pltpu.make_async_remote_copy(
            src_ref=source, dst_ref=target, send_sem=send, recv_sem=recv,
            device_id=(to_lon, to_lat, to_ch), device_id_type=MESH,
        )

    barrier = pltpu.get_barrier_semaphore()

    def greet(to_lon, to_lat, to_ch):
        pl.semaphore_signal(barrier, inc=1, device_id=(to_lon, to_lat, to_ch), device_id_type=MESH)

    for i in range(1, 16):
        greet(lax.rem(lon + i, 16), lat, ch)
        greet(lax.rem(lon + i, 16), lat, other)
    greet(lon, lat, other)
    for i in range(1, 8):
        greet(lon, lax.rem(lat + i, 8), ch)

    @pl.when(lat > 0)
    def _():
        greet(lax.rem(lon + 1, 16), lat - 1, ch)
        greet(lax.rem(lon + 15, 16), lat - 1, ch)

    @pl.when(lat < 7)
    def _():
        greet(lax.rem(lon + 1, 16), lat + 1, ch)
        greet(lax.rem(lon + 15, 16), lat + 1, ch)

    field_copy = pltpu.make_async_copy(t_ref, narrow, loc.at[0])
    field_copy.start()

    own_half = pl.ds(pl.multiple_of(64 * ch, 64), 64)
    for da in range(3):
        gap = jnp.zeros((64, CP - 69), F32)
        parts = []
        for db in range(3):
            parts += [wc_ref[3 * da + db].astype(F32), gap]
        wc[da, own_half] = jnp.concatenate(parts + [jnp.zeros((64, 16), F32)], axis=1).astype(BF)
    w_copies = [
        pltpu.make_async_copy(w_ref.at[:, pl.ds(1024 * s, 1024)], wv.at[s], loc.at[2 + s]) for s in range(16)
    ]
    for c in w_copies:
        c.start()

    j = lax.broadcasted_iota(jnp.int32, (1, 768), 1)
    column = 4 * (j % 32) + j // 128 - 1
    target = jnp.where((column >= 0) & (column < 128), column + 128 * ((j % 128) // 32), -1)
    p1[...] = one_hot(target, 512)
    xs[:, 480:496, :] = jnp.zeros((6, 16, 256), BF)
    cga[...] = jnp.zeros_like(cga)

    wide[4416:5120] = jnp.zeros((704, 128), F32)
    field_copy.wait()

    def widen(c, _):
        wide[pl.ds(pl.multiple_of(64 * c, 64), 64)] = narrow[c].astype(F32)
        return 0

    lax.fori_loop(0, 69, widen, 0, unroll=23)
    edge[...] = wide[pl.ds(63 * other, CP, stride=64)].astype(BF)
    lane = lax.broadcasted_iota(jnp.int32, (CP, 128), 1)
    left = jnp.zeros((CP, 128), F32)
    right = jnp.zeros((CP, 128), F32)
    for m in range(33):
        row = wide[pl.ds(31 * ch + m, CP, stride=64)]
        slab[other + m] = row.astype(BF)
        if m:
            row = pltpu.roll(row, m, 1)
        left = jnp.where(lane == (m + 127) % 128, row, left)
        right = jnp.where(lane == m, row, right)
    pack_l[...] = left.astype(BF)
    pack_r[...] = right.astype(BF)
    @pl.when((lat == 0) | (lat == 7))
    def _():
        pl.semaphore_wait(barrier, 40)

    @pl.when((lat > 0) & (lat < 7))
    def _():
        pl.semaphore_wait(barrier, 42)

    def halo_copies(to_lat, base):
        out = []
        for n, (shift, target) in enumerate(((0, slab.at[33 * ch]), (1, halo_l), (15, halo_r))):
            to = lax.rem(base + shift, 16)
            out.append(remote(edge, target, ha_s.at[n], ha_r.at[n], to, to_lat, ch))
        return out

    inner = halo_copies(lat + 1 - 2 * ch, lon)
    polar_s = []
    for n, (shift, target) in enumerate(((0, slab.at[33 * ch]), (1, halo_l), (15, halo_r))):
        to = lax.rem(lon + 8 + shift, 16)
        polar_s.append(remote(slab.at[1 + 31 * ch], target, ha_s.at[3 + n], ha_r.at[n], to, lat, ch))
    has_inner = lat != 7 * other
    has_polar = lat == 7 * ch

    @pl.when(has_inner)
    def _():
        for c in inner:
            c.start()

    @pl.when(has_polar)
    def _():
        for c in polar_s:
            c.start()

    pk0 = remote(pack_l, got_l, pk_s.at[0], pk_r.at[0], lax.rem(lon + 1, 16), lat, ch)
    pk1 = remote(pack_r, got_r, pk_s.at[1], pk_r.at[1], lax.rem(lon + 15, 16), lat, ch)
    pk0.start()
    pk1.start()

    wc_remote = remote(wc.at[:, own_half], wc.at[:, own_half], wc_s, wc_r, lon, lat, other)
    wc_remote.start()

    tg_copies = []
    for i in range(8):
        to = 8 * ch + lax.rem(lo + i, 8)
        rows = pl.ds(pl.multiple_of(32 * to, 32), 32)
        place = pl.ds(pl.multiple_of(32 * lo, 32), 32)
        tg_copies.append(remote(tg_ref.at[rows], tgo.at[place], tg_s.at[i], tg_r.at[i], to, lat, hi))
    tg_own = pltpu.make_async_copy(tg_ref.at[pl.ds(pl.multiple_of(32 * lon, 32), 32)], tgo.at[place], tg_r.at[0])
    for i in (4, 3, 5, 2, 6, 1, 7):
        tg_copies[i].start()

    @pl.when(ch == hi)
    def _():
        tg_own.start()

    @pl.when(ch != hi)
    def _():
        tg_copies[0].start()

    for c in inner:
        c.wait_recv()

    def gather_rows(u, _):
        for half in range(2):
            for k in range(4):
                src[u, pl.ds(CP * half, CP), 128 * k : 128 * k + 128] = slab[16 * half + 4 * k + u]
        return 0

    lax.fori_loop(0, 6, gather_rows, 0, unroll=2)
    pk0.wait_recv()
    pk1.wait_recv()
    edges = jnp.concatenate([got_l[...], got_r[...], halo_l[...], halo_r[...]], axis=1)
    j2 = lax.broadcasted_iota(jnp.int32, (1, 256), 1)
    side = j2 // 128
    at_edge = (j2 % 32) == 31 * side

    def depth(u, _):
        res = dot(src[u], p1[...])
        for half in range(2):
            row = 16 * half + u + 4 * ((j2 % 128) // 32)
            m = row - other
            own = jnp.where(side == 0, (m + 127) % 128, 128 + m)
            want = jnp.where(row == 33 * ch, jnp.where(side == 0, 256 + 127, 384), own)
            fill = dot(edges, one_hot(jnp.where(at_edge, want, -1), 512))
            part = res[CP * half : CP * half + CP]
            lanes = slice(128 * half, 128 * half + 128)
            xs[u, 0:CP, lanes] = (part[:, 0:128] + fill[:, 0:128]).astype(BF)
            for v in range(1, 5):
                xs[u, CP * v : CP * v + CP, lanes] = part[:, 128 * v : 128 * v + 128].astype(BF)
            xs[u, CP * 5 : CP * 6, lanes] = (part[:, 640:768] + fill[:, 128:256]).astype(BF)
        return 0

    lax.fori_loop(0, 6, depth, 0, unroll=2)

    wc_remote.wait_recv()

    def conv(s, _):
        a = s // 4
        first = pl.multiple_of(CP * (s % 4), 16)
        v = jnp.zeros((128, 256), F32)
        for da in range(3):
            v = v + dot(wc[da], xs[a + da, pl.ds(first, 256), :])
        root = 0.7978845608028654
        square = v * v
        th = jnp.tanh(root * v * (1.0 + 0.044715 * square))
        half = 0.5 * (1.0 + th)
        slope = half + 0.5 * v * (1.0 - th * th) * (root * (1.0 + 3 * 0.044715 * square))
        h = (v * half).astype(BF)
        dgelu[s] = slope
        hid[s] = h.reshape(2, 64, 256)
        hidt[:, pl.ds(pl.multiple_of(128 * s, 128), 128)] = h.T
        return 0

    lax.fori_loop(0, 16, conv, 0, unroll=4)
    hp = remote(hid.at[:, other], hidp, hp_s, hp_r, lon, lat, other)
    hp.start()
    for c in w_copies:
        c.wait()

    def embed(n, _):
        columns = pl.ds(pl.multiple_of(256 * n, 256), 256)
        part = jnp.zeros((256, 256), F32)
        for s in range(16):
            part = part + dot(hidt[:, 128 * s : 128 * s + 128], wv[s, :, columns])
        emb[n // 2, :, pl.ds(pl.multiple_of(256 * (n % 2), 256), 256)] = part.astype(BF)
        return 0

    lax.fori_loop(0, 4, embed, 0, unroll=2)
    emb_copies = {}
    for i in (4, 3, 5, 2, 6, 1, 7, 0):
        r = lax.rem(lo + i, 8)
        for g in range(2):
            emb_copies[i, g] = remote(
                emb.at[g, pl.ds(pl.multiple_of(32 * r, 32), 32)],
                emb_out.at[pl.ds(pl.multiple_of(32 * lon, 32), 32)],
                em_s.at[2 * i + g], em_r.at[2 * i + hi], 8 * ch + r, lat, g,
            )
            if i:
                emb_copies[i, g].start()
            else:
                mine = (ch == hi) & (ch == g)

                @pl.when(mine)
                def _(g=g):
                    pltpu.make_async_copy(
                        emb.at[g, pl.ds(pl.multiple_of(32 * lo, 32), 32)],
                        emb_out.at[pl.ds(pl.multiple_of(32 * lon, 32), 32)],
                        em_r.at[hi],
                    ).start()

                @pl.when(jnp.logical_not(mine))
                def _(g=g):
                    emb_copies[0, g].start()

    def ya_copy(cc, n):
        return remote(
            ysb.at[cc, n - 1], yrb.at[cc, n - 1], a_s.at[cc, n - 1], a_r.at[cc, n - 1],
            lon, lax.rem(lat + 2 * n, 8), ch,
        )

    def yb_copy(cc):
        return remote(yxs.at[cc], yxr.at[cc], b_s.at[cc], b_r.at[cc], lon, lat + 1 - 2 * xlo, ch)

    def xa_copy(cc):
        return remote(xsb.at[cc], xrb.at[cc], xa_s.at[cc], xa_r.at[cc], lon, lat + 1 - 2 * xlo, ch)

    def xb_copy(cc, n):
        return remote(
            xys.at[cc, n - 1], xyr.at[cc, n - 1], xb_s.at[cc, n - 1], xb_r.at[cc, n - 1],
            lon, lax.rem(lat + 2 * n, 8), ch,
        )

    def split(value):
        first, second = value[:, 0:128], value[:, 128:256]
        return jnp.where(xlo == 0, first, second), jnp.where(xlo == 0, second, first)

    def eg_part(chunk, n):
        columns = pl.ds(pl.multiple_of(256 * lax.rem(y + n, 4), 256), 256)
        mine = hid[4 * chunk : 4 * chunk + 4, ch].reshape(256, 256)
        theirs = hidp[4 * chunk : 4 * chunk + 4].reshape(256, 256)
        return dot(mine, tgo[:, columns]) + dot(theirs, tgp[:, columns])

    def stage_yb(cc):
        total = yown[cc]
        for n in (1, 3, 2):
            ya_copy(cc, n).wait_recv()
            total = total + yrb[cc, n - 1].astype(F32)
        mine, theirs = split(total)
        ycf[cc] = mine
        yxs[cc] = theirs.astype(BF)
        yb_copy(cc).start()

    def stage_xb(cc):
        xa_copy(cc).wait_recv()
        xcf[cc] = xown[cc, :, 0:128] + xrb[cc, :, 0:128].astype(F32)
        for n in (2, 1, 3):
            lanes = slice(128 * n, 128 * n + 128)
            xys[cc, n - 1] = (xown[cc, :, lanes] + xrb[cc, :, lanes].astype(F32)).astype(BF)
            xb_copy(cc, n).start()

    def c_copy(s):
        i = lax.rem(s - lon + 16, 16)
        return remote(scb.at[s], rc.at[i], c_s.at[i], c_r.at[i], s, lat, ch)

    def stage_c(chunk):
        if chunk < 2:
            yb_copy(chunk).wait_recv()
            total = ycf[chunk] + yxr[chunk].astype(F32)
        else:
            total = xcf[chunk - 2]
            for n in (1, 3, 2):
                xb_copy(chunk - 2, n).wait_recv()
                total = total + xyr[chunk - 2, n - 1].astype(F32)
        total = total.reshape(4, 64, 128)
        scf[4 * chunk : 4 * chunk + 4] = total
        scb[4 * chunk : 4 * chunk + 4] = total.astype(BF)
        for s in range(4 * chunk, 4 * chunk + 4):

            @pl.when(s != lon)
            def _(s=s):
                c_copy(s).start()

    forwards = []
    for i in (0, 1, 7, 2, 6, 3, 5, 4):
        tg_copies[i].wait_recv()
        rows = pl.ds(pl.multiple_of(32 * lax.rem(lo + 8 - i, 8), 32), 32)
        forwards.append(remote(tgo.at[rows], tgp.at[rows], tf_s.at[i], tf_r.at[lax.rem(lo + 8 - i, 8)], lon, lat, other))
        forwards[-1].start()
    hp.wait_recv()
    for c in forwards:
        c.wait_recv()
    for cc in range(2):
        for n in range(4):
            mine, theirs = split(eg_part(2 + cc, n))
            lanes = slice(128 * n, 128 * n + 128)
            xown[cc, :, lanes] = mine
            xsb[cc, :, lanes] = theirs.astype(BF)
        xa_copy(cc).start()
        for n in (2, 1, 3):
            ysb[cc, n - 1] = eg_part(cc, n).astype(BF)
            ya_copy(cc, n).start()
        yown[cc] = eg_part(cc, 0)

    def conv_grad(a, _):
        hg = dot(wv[pl.ds(4 * a, 4)].reshape(512, 1024), tgo[...], NT)
        pg = (hg * dgelu[pl.ds(4 * a, 4)].reshape(512, 256)).astype(BF)
        for da in range(3):
            total = cga[da]
            for b in range(4):
                total = total + dot(pg[128 * b : 128 * b + 128], xs[a + da, CP * b : CP * b + 256, :], NT)
            cga[da] = total
        return 0

    lax.fori_loop(0, 4, conv_grad, 0, unroll=4)
    half_o = pl.ds(pl.multiple_of(64 * other, 64), 64)
    q_copy = remote(cga.at[:, half_o, :], cgp, q_s, q_r, lon, lat, other)
    q_copy.start()

    def d_copy(j):
        i = lax.rem(j - lon + 16, 16)
        return remote(scb16.at[j], rcg.at[i], d_s.at[j], d_r.at[i], j, lat, ch)

    def e_copy(i):
        return remote(l0, rl.at[lat], e_s.at[i], e_r.at[i], lon, lax.rem(lat + i, 8), ch)

    def f_copy(i):
        return remote(l1, agb.at[lon], f_s.at[i], f_r.at[lon], lax.rem(lon + i, 16), lat, ch)

    q_copy.wait_recv()
    total = cga[:, pl.ds(pl.multiple_of(64 * ch, 64), 64), :] + cgp[...]
    for j in range(12):
        for half in range(2):
            piece = total[j // 4, 16 * (j % 4) : 16 * (j % 4) + 16, 128 * half : 128 * half + 128]
            scg[j, half] = piece
            scb16[j, half] = piece.astype(BF)
    for j in range(12):

        @pl.when(j != lon)
        def _(j=j):
            d_copy(j).start()

    stage_xb(0)
    stage_yb(0)
    stage_xb(1)
    stage_yb(1)

    @pl.when(lon < 12)
    def _():
        total = scg[lon]
        for i in range(1, 16):
            remote(scb16.at[0], rcg.at[i], d_s.at[0], d_r.at[i], lon, lat, other).wait_recv()
            total = total + rcg[i].astype(F32)
        l0[...] = total
        rl[lat] = total
        for i in range(1, 8):
            e_copy(i).start()

    stage_c(0)
    stage_c(2)
    stage_c(1)

    @pl.when(lon < 12)
    def _():
        for i in range(1, 8):
            e_copy(i).wait_recv()
        total = rl[0]
        for i in range(1, 8):
            total = total + rl[i]
        total = total.astype(BF)
        l1[...] = total
        agb[lon] = total
        for i in range(1, 16):
            f_copy(i).start()

    stage_c(3)
    total = scf[lon]
    for i in range(1, 16):
        remote(scb.at[0], rc.at[i], c_s.at[i], c_r.at[i], lon, lat, other).wait_recv()
        total = total + rc[i].astype(F32)
    eg_out[...] = total

    for j in range(12):

        @pl.when(j != lon)
        def _(j=j):
            remote(l1, agb.at[j], f_s.at[0], f_r.at[j], lon, lat, other).wait_recv()

        for half in range(2):
            full[j // 4, 16 * (j % 4) : 16 * (j % 4) + 16, 128 * half : 128 * half + 128] = agb[j, half].astype(F32)
    for da in range(3):
        for db in range(3):
            cg_out[3 * da + db] = full[da, :, CP * db : CP * db + 69]

    for i in range(8):
        for g in range(2):
            remote(
                emb.at[0, pl.ds(0, 32)], emb_out.at[pl.ds(0, 32)],
                em_s.at[0], em_r.at[2 * i + g], lon, lat, other,
            ).wait_recv()

    @pl.when(has_inner)
    def _():
        for c in inner:
            c.wait_send()

    @pl.when(has_polar)
    def _():
        for c in polar_s:
            c.wait_send()

    wc_remote.wait_send()
    for i in range(1, 8):
        tg_copies[i].wait_send()

    @pl.when(ch != hi)
    def _():
        tg_copies[0].wait_send()

    pk0.wait_send()
    pk1.wait_send()
    hp.wait_send()
    q_copy.wait_send()
    for c in forwards:
        c.wait_send()
    for (i, g), c in emb_copies.items():
        if i:
            c.wait_send()
        else:

            @pl.when(jnp.logical_not((ch == hi) & (ch == g)))
            def _(c=c):
                c.wait_send()

    for cc in range(2):
        for n in (1, 2, 3):
            ya_copy(cc, n).wait_send()
            xb_copy(cc, n).wait_send()
        yb_copy(cc).wait_send()
        xa_copy(cc).wait_send()
    for i in range(1, 16):
        remote(scb.at[0], rc.at[i], c_s.at[i], c_r.at[i], lon, lat, other).wait_send()
    for j in range(12):

        @pl.when(j != lon)
        def _(j=j):
            d_copy(j).wait_send()

    @pl.when(lon < 12)
    def _():
        for i in range(1, 16):
            f_copy(i).wait_send()
        for i in range(1, 8):
            e_copy(i).wait_send()


def step(t, wc, w, tg):
    vm = pltpu.VMEM
    sem = pltpu.SemaphoreType.DMA
    scratch = [
        vm((69, 64, 128), BF), vm((64 * CP, 128), F32), vm((CP, 128), BF), vm((34, CP, 128), BF), vm((CP, 128), BF), vm((CP, 128), BF), vm((CP, 128), BF), vm((CP, 128), BF),
        vm((CP, 128), BF), vm((CP, 128), BF),
        vm((3, 128, 256), BF), vm((16, 128, 1024), BF), vm((256, 1024), BF), vm((256, 1024), BF),
        vm((6, 2 * CP, 512), BF), vm((512, 768), BF), vm((6, 496, 256), BF),
        vm((16, 2, 64, 256), BF), vm((16, 64, 256), BF), vm((256, 2048), BF), vm((16, 128, 256), F32),
        vm((2, 256, 512), BF),
        vm((2, 3, 256, 256), BF), vm((2, 3, 256, 256), BF), vm((2, 256, 256), F32),
        vm((2, 256, 128), BF), vm((2, 256, 128), BF), vm((2, 256, 128), F32),
        vm((2, 256, 512), BF), vm((2, 256, 512), BF), vm((2, 256, 512), F32),
        vm((2, 3, 256, 128), BF), vm((2, 3, 256, 128), BF), vm((2, 256, 128), F32),
        vm((16, 64, 128), F32), vm((16, 64, 128), BF), vm((16, 64, 128), BF),
        vm((3, 128, 256), F32), vm((3, 64, 256), F32), vm((12, 2, 16, 128), F32), vm((12, 2, 16, 128), BF),
        vm((16, 2, 16, 128), BF), vm((2, 16, 128), F32), vm((8, 2, 16, 128), F32), vm((2, 16, 128), BF),
        vm((12, 2, 16, 128), BF), vm((3, 64, 256), F32),
        sem((18,)), sem((8,)), sem((8,)), sem((6,)), sem((3,)), sem((2,)), sem((2,)), sem, sem,
        sem((16,)), sem((16,)), sem((8,)), sem((8,)), sem, sem,
        sem((2, 3)), sem((2, 3)), sem((2,)), sem((2,)), sem((2,)), sem((2,)), sem((2, 3)), sem((2, 3)), sem((16,)), sem((16,)), sem, sem,
        sem((12,)), sem((16,)), sem((8,)), sem((8,)), sem((16,)), sem((12,)),
    ]
    any_ = pl.BlockSpec(memory_space=pl.ANY)
    inside = pl.BlockSpec(memory_space=pltpu.VMEM)
    return pl.pallas_call(
        kernel,
        out_shape=(
            jax.ShapeDtypeStruct((512, 512), BF),
            jax.ShapeDtypeStruct((64, 128), F32),
            jax.ShapeDtypeStruct((9, 64, 69), F32),
        ),
        in_specs=[any_, inside, any_, any_],
        out_specs=(any_, inside, inside),
        scratch_shapes=scratch,
        compiler_params=pltpu.CompilerParams(vmem_limit_bytes=56 * 1024 * 1024, has_side_effects=True, collective_id=0),
    )(t, wc, w, tg)


def settle(emb, eg, cg, emb_out, eg_out, cg_out, emb_held, eg_held, cg_held, sem):
    moves = []
    for n in range(4):
        rows = pl.ds(128 * n, 128)
        moves.append((emb.at[rows], emb_held.at[rows], emb_out.at[rows]))
    moves += [(eg, eg_held, eg_out), (cg, cg_held, cg_out)]
    moves = [
        (pltpu.make_async_copy(a, b, sem.at[0, n]), pltpu.make_async_copy(b, c, sem.at[1, n]))
        for n, (a, b, c) in enumerate(moves)
    ]
    for first, _ in moves:
        first.start()
    for first, second in moves:
        first.wait()
        second.start()
    for _, second in moves:
        second.wait()


def body(fields, conv_weight, embed_weight, token_grads):
    embedded, embed_gradient, conv_gradient = step(fields, conv_weight.transpose(1, 0, 2), embed_weight, token_grads.reshape(512, 1024))
    shapes = [(a.shape, a.dtype) for a in (embedded, embed_gradient, conv_gradient)]
    outside = pl.BlockSpec(memory_space=pltpu.HBM)
    embedded, embed_gradient, conv_gradient = pl.pallas_call(
        settle,
        out_shape=tuple(jax.ShapeDtypeStruct(*a) for a in shapes),
        in_specs=[outside] * 3,
        out_specs=(outside,) * 3,
        scratch_shapes=[pltpu.VMEM(*a) for a in shapes] + [pltpu.SemaphoreType.DMA((2, 6))],
    )(embedded, embed_gradient, conv_gradient)
    return embedded.reshape(1, 1, 512, 512), conv_gradient.transpose(1, 0, 2), embed_gradient


def solution(mesh):
    return jax.shard_map(
        body,
        mesh=mesh,
        in_specs=(P(None, "lat", "lon"), P("ch", None, None), P(), P("lon", "lat", None, None)),
        out_specs=(P("lon", "lat", None, "ch"), P("ch", None, None), P("ch", ("lon", "lat"))),
        check_vma=False,
    )
```

```python
import functools

import jax
import jax.numpy as jnp
from jax import lax
from jax.experimental import pallas as pl
from jax.experimental.pallas import tpu as pltpu
from jax.sharding import PartitionSpec as P

BF = jnp.bfloat16
F32 = jnp.float32
MESH = pl.DeviceIdType.MESH
CP = 80
NN = (((1,), (0,)), ((), ()))
NT = (((1,), (1,)), ((), ()))


def dot(x, y, dims=NN):
    return lax.dot_general(x, y, dims, preferred_element_type=F32)


def one_hot(target, rows):
    index = lax.broadcasted_iota(jnp.int32, (rows, target.shape[1]), 0)
    return jnp.where(index == target, 1.0, 0.0).astype(BF)


def kernel(
    t_ref, wc_ref, w_ref, tg_ref,
    emb_out, eg_out, cg_out,
    narrow, wide, edge, slab, halo_l, halo_r, got_l, got_r, pack_l, pack_r,
    wc, wv, tgo, tgp, src, p1, xs, hid, hidp, hidt, dgelu, emb,
    ysb, yrb, yown, yxs, yxr, ycf, xsb, xrb, xown, xys, xyr, xcf, scf, scb, rc,
    cga, cgp, scg, scb16, rcg, l0, rl, l1, agb, full,
    loc, tg_s, tg_r, ha_s, ha_r, pk_s, pk_r, wc_s, wc_r, em_s, em_r, tf_s, tf_r, hp_s, hp_r,
    a_s, a_r, b_s, b_r, xa_s, xa_r, xb_s, xb_r, c_s, c_r, q_s, q_r, d_s, d_r, e_s, e_r, f_s, f_r,
):
    lon = lax.axis_index("lon")
    lat = lax.axis_index("lat")
    ch = lax.axis_index("ch")
    hi = lon // 8
    lo = lax.rem(lon, 8)
    y = lat // 2
    xlo = lax.rem(lat, 2)
    other = 1 - ch

    def remote(source, target, send, recv, to_lon, to_lat, to_ch):
        return pltpu.make_async_remote_copy(
            src_ref=source, dst_ref=target, send_sem=send, recv_sem=recv,
            device_id=(to_lon, to_lat, to_ch), device_id_type=MESH,
        )

    barrier = pltpu.get_barrier_semaphore()

    def greet(to_lon, to_lat, to_ch):
        pl.semaphore_signal(barrier, inc=1, device_id=(to_lon, to_lat, to_ch), device_id_type=MESH)

    for i in range(1, 16):
        greet(lax.rem(lon + i, 16), lat, ch)
        greet(lax.rem(lon + i, 16), lat, other)
    greet(lon, lat, other)
    for i in range(1, 8):
        greet(lon, lax.rem(lat + i, 8), ch)

    @pl.when(lat > 0)
    def _():
        greet(lax.rem(lon + 1, 16), lat - 1, ch)
        greet(lax.rem(lon + 15, 16), lat - 1, ch)

    @pl.when(lat < 7)
    def _():
        greet(lax.rem(lon + 1, 16), lat + 1, ch)
        greet(lax.rem(lon + 15, 16), lat + 1, ch)

    field_copy = pltpu.make_async_copy(t_ref, narrow, loc.at[0])
    field_copy.start()

    own_half = pl.ds(pl.multiple_of(64 * ch, 64), 64)
    for da in range(3):
        gap = jnp.zeros((64, CP - 69), F32)
        parts = []
        for db in range(3):
            parts += [wc_ref[3 * da + db].astype(F32), gap]
        wc[da, own_half] = jnp.concatenate(parts + [jnp.zeros((64, 16), F32)], axis=1).astype(BF)
    w_copies = [
        pltpu.make_async_copy(w_ref.at[:, pl.ds(1024 * s, 1024)], wv.at[s], loc.at[2 + s]) for s in range(16)
    ]
    for c in w_copies:
        c.start()

    j = lax.broadcasted_iota(jnp.int32, (1, 768), 1)
    column = 4 * (j % 32) + j // 128 - 1
    target = jnp.where((column >= 0) & (column < 128), column + 128 * ((j % 128) // 32), -1)
    p1[...] = one_hot(target, 512)
    xs[:, 480:496, :] = jnp.zeros((6, 16, 256), BF)
    cga[...] = jnp.zeros_like(cga)

    wide[4416:5120] = jnp.zeros((704, 128), F32)
    field_copy.wait()

    def widen(c, _):
        wide[pl.ds(pl.multiple_of(64 * c, 64), 64)] = narrow[c].astype(F32)
        return 0

    lax.fori_loop(0, 69, widen, 0, unroll=23)
    edge[...] = wide[pl.ds(63 * other, CP, stride=64)].astype(BF)
    lane = lax.broadcasted_iota(jnp.int32, (CP, 128), 1)
    left = jnp.zeros((CP, 128), F32)
    right = jnp.zeros((CP, 128), F32)
    for m in range(33):
        row = wide[pl.ds(31 * ch + m, CP, stride=64)]
        slab[other + m] = row.astype(BF)
        if m:
            row = pltpu.roll(row, m, 1)
        left = jnp.where(lane == (m + 127) % 128, row, left)
        right = jnp.where(lane == m, row, right)
    pack_l[...] = left.astype(BF)
    pack_r[...] = right.astype(BF)
    @pl.when((lat == 0) | (lat == 7))
    def _():
        pl.semaphore_wait(barrier, 40)

    @pl.when((lat > 0) & (lat < 7))
    def _():
        pl.semaphore_wait(barrier, 42)

    def halo_copies(to_lat, base):
        out = []
        for n, (shift, target) in enumerate(((0, slab.at[33 * ch]), (1, halo_l), (15, halo_r))):
            to = lax.rem(base + shift, 16)
            out.append(remote(edge, target, ha_s.at[n], ha_r.at[n], to, to_lat, ch))
        return out

    inner = halo_copies(lat + 1 - 2 * ch, lon)
    polar_s = []
    for n, (shift, target) in enumerate(((0, slab.at[33 * ch]), (1, halo_l), (15, halo_r))):
        to = lax.rem(lon + 8 + shift, 16)
        polar_s.append(remote(slab.at[1 + 31 * ch], target, ha_s.at[3 + n], ha_r.at[n], to, lat, ch))
    has_inner = lat != 7 * other
    has_polar = lat == 7 * ch

    @pl.when(has_inner)
    def _():
        for c in inner:
            c.start()

    @pl.when(has_polar)
    def _():
        for c in polar_s:
            c.start()

    pk0 = remote(pack_l, got_l, pk_s.at[0], pk_r.at[0], lax.rem(lon + 1, 16), lat, ch)
    pk1 = remote(pack_r, got_r, pk_s.at[1], pk_r.at[1], lax.rem(lon + 15, 16), lat, ch)
    pk0.start()
    pk1.start()

    wc_remote = remote(wc.at[:, own_half], wc.at[:, own_half], wc_s, wc_r, lon, lat, other)
    wc_remote.start()

    tg_copies = []
    for i in range(8):
        to = 8 * ch + lax.rem(lo + i, 8)
        rows = pl.ds(pl.multiple_of(32 * to, 32), 32)
        place = pl.ds(pl.multiple_of(32 * lo, 32), 32)
        tg_copies.append(remote(tg_ref.at[rows], tgo.at[place], tg_s.at[i], tg_r.at[i], to, lat, hi))
    tg_own = pltpu.make_async_copy(tg_ref.at[pl.ds(pl.multiple_of(32 * lon, 32), 32)], tgo.at[place], tg_r.at[0])
    for i in (4, 3, 5, 2, 6, 1, 7):
        tg_copies[i].start()

    @pl.when(ch == hi)
    def _():
        tg_own.start()

    @pl.when(ch != hi)
    def _():
        tg_copies[0].start()

    for c in inner:
        c.wait_recv()

    def gather_rows(u, _):
        for half in range(2):
            for k in range(4):
                src[u, pl.ds(CP * half, CP), 128 * k : 128 * k + 128] = slab[16 * half + 4 * k + u]
        return 0

    lax.fori_loop(0, 6, gather_rows, 0, unroll=2)
    pk0.wait_recv()
    pk1.wait_recv()
    edges = jnp.concatenate([got_l[...], got_r[...], halo_l[...], halo_r[...]], axis=1)
    j2 = lax.broadcasted_iota(jnp.int32, (1, 256), 1)
    side = j2 // 128
    at_edge = (j2 % 32) == 31 * side

    def depth(u, _):
        res = dot(src[u], p1[...])
        for half in range(2):
            row = 16 * half + u + 4 * ((j2 % 128) // 32)
            m = row - other
            own = jnp.where(side == 0, (m + 127) % 128, 128 + m)
            want = jnp.where(row == 33 * ch, jnp.where(side == 0, 256 + 127, 384), own)
            fill = dot(edges, one_hot(jnp.where(at_edge, want, -1), 512))
            part = res[CP * half : CP * half + CP]
            lanes = slice(128 * half, 128 * half + 128)
            xs[u, 0:CP, lanes] = (part[:, 0:128] + fill[:, 0:128]).astype(BF)
            for v in range(1, 5):
                xs[u, CP * v : CP * v + CP, lanes] = part[:, 128 * v : 128 * v + 128].astype(BF)
            xs[u, CP * 5 : CP * 6, lanes] = (part[:, 640:768] + fill[:, 128:256]).astype(BF)
        return 0

    lax.fori_loop(0, 6, depth, 0, unroll=2)

    wc_remote.wait_recv()

    def conv(s, _):
        a = s // 4
        first = pl.multiple_of(CP * (s % 4), 16)
        v = jnp.zeros((128, 256), F32)
        for da in range(3):
            v = v + dot(wc[da], xs[a + da, pl.ds(first, 256), :])
        root = 0.7978845608028654
        square = v * v
        th = jnp.tanh(root * v * (1.0 + 0.044715 * square))
        half = 0.5 * (1.0 + th)
        slope = half + 0.5 * v * (1.0 - th * th) * (root * (1.0 + 3 * 0.044715 * square))
        h = (v * half).astype(BF)
        dgelu[s] = slope
        hid[s] = h.reshape(2, 64, 256)
        hidt[:, pl.ds(pl.multiple_of(128 * s, 128), 128)] = h.T
        return 0

    lax.fori_loop(0, 16, conv, 0, unroll=4)
    hp = remote(hid.at[:, other], hidp, hp_s, hp_r, lon, lat, other)
    hp.start()
    for c in w_copies:
        c.wait()

    def embed(n, _):
        columns = pl.ds(pl.multiple_of(256 * n, 256), 256)
        part = jnp.zeros((256, 256), F32)
        for s in range(16):
            part = part + dot(hidt[:, 128 * s : 128 * s + 128], wv[s, :, columns])
        emb[n // 2, :, pl.ds(pl.multiple_of(256 * (n % 2), 256), 256)] = part.astype(BF)
        return 0

    lax.fori_loop(0, 4, embed, 0, unroll=2)
    emb_copies = {}
    for i in (1, 7, 4, 2, 6, 3, 5, 0):
        r = lax.rem(lo + i, 8)
        for g in range(2):
            emb_copies[i, g] = remote(
                emb.at[g, pl.ds(pl.multiple_of(32 * r, 32), 32)],
                emb_out.at[pl.ds(pl.multiple_of(32 * lon, 32), 32)],
                em_s.at[2 * i + g], em_r.at[2 * i + hi], 8 * ch + r, lat, g,
            )
            if i:
                emb_copies[i, g].start()
            else:
                mine = (ch == hi) & (ch == g)

                @pl.when(mine)
                def _(g=g):
                    pltpu.make_async_copy(
                        emb.at[g, pl.ds(pl.multiple_of(32 * lo, 32), 32)],
                        emb_out.at[pl.ds(pl.multiple_of(32 * lon, 32), 32)],
                        em_r.at[hi],
                    ).start()

                @pl.when(jnp.logical_not(mine))
                def _(g=g):
                    emb_copies[0, g].start()

    def ya_copy(cc, n):
        return remote(
            ysb.at[cc, n - 1], yrb.at[cc, n - 1], a_s.at[cc, n - 1], a_r.at[cc, n - 1],
            lon, lax.rem(lat + 2 * n, 8), ch,
        )

    def yb_copy(cc):
        return remote(yxs.at[cc], yxr.at[cc], b_s.at[cc], b_r.at[cc], lon, lat + 1 - 2 * xlo, ch)

    def xa_copy(cc):
        return remote(xsb.at[cc], xrb.at[cc], xa_s.at[cc], xa_r.at[cc], lon, lat + 1 - 2 * xlo, ch)

    def xb_copy(cc, n):
        return remote(
            xys.at[cc, n - 1], xyr.at[cc, n - 1], xb_s.at[cc, n - 1], xb_r.at[cc, n - 1],
            lon, lax.rem(lat + 2 * n, 8), ch,
        )

    def split(value):
        first, second = value[:, 0:128], value[:, 128:256]
        return jnp.where(xlo == 0, first, second), jnp.where(xlo == 0, second, first)

    def eg_part(chunk, n):
        columns = pl.ds(pl.multiple_of(256 * lax.rem(y + n, 4), 256), 256)
        mine = hid[4 * chunk : 4 * chunk + 4, ch].reshape(256, 256)
        theirs = hidp[4 * chunk : 4 * chunk + 4].reshape(256, 256)
        return dot(mine, tgo[:, columns]) + dot(theirs, tgp[:, columns])

    def stage_yb(cc):
        total = yown[cc]
        for n in (1, 3, 2):
            ya_copy(cc, n).wait_recv()
            total = total + yrb[cc, n - 1].astype(F32)
        mine, theirs = split(total)
        ycf[cc] = mine
        yxs[cc] = theirs.astype(BF)
        yb_copy(cc).start()

    def stage_xb(cc):
        xa_copy(cc).wait_recv()
        xcf[cc] = xown[cc, :, 0:128] + xrb[cc, :, 0:128].astype(F32)
        for n in (2, 1, 3):
            lanes = slice(128 * n, 128 * n + 128)
            xys[cc, n - 1] = (xown[cc, :, lanes] + xrb[cc, :, lanes].astype(F32)).astype(BF)
            xb_copy(cc, n).start()

    def c_copy(s):
        i = lax.rem(s - lon + 16, 16)
        return remote(scb.at[s], rc.at[i], c_s.at[i], c_r.at[i], s, lat, ch)

    def stage_c(chunk):
        if chunk < 2:
            yb_copy(chunk).wait_recv()
            total = ycf[chunk] + yxr[chunk].astype(F32)
        else:
            total = xcf[chunk - 2]
            for n in (1, 3, 2):
                xb_copy(chunk - 2, n).wait_recv()
                total = total + xyr[chunk - 2, n - 1].astype(F32)
        total = total.reshape(4, 64, 128)
        scf[4 * chunk : 4 * chunk + 4] = total
        scb[4 * chunk : 4 * chunk + 4] = total.astype(BF)
        for s in range(4 * chunk, 4 * chunk + 4):

            @pl.when(s != lon)
            def _(s=s):
                c_copy(s).start()

    forwards = []
    for i in (0, 1, 7, 2, 6, 3, 5, 4):
        tg_copies[i].wait_recv()
        rows = pl.ds(pl.multiple_of(32 * lax.rem(lo + 8 - i, 8), 32), 32)
        forwards.append(remote(tgo.at[rows], tgp.at[rows], tf_s.at[i], tf_r.at[lax.rem(lo + 8 - i, 8)], lon, lat, other))
        forwards[-1].start()
    hp.wait_recv()
    for c in forwards:
        c.wait_recv()
    for cc in range(2):
        for n in range(4):
            mine, theirs = split(eg_part(2 + cc, n))
            lanes = slice(128 * n, 128 * n + 128)
            xown[cc, :, lanes] = mine
            xsb[cc, :, lanes] = theirs.astype(BF)
        xa_copy(cc).start()
        for n in (2, 1, 3):
            ysb[cc, n - 1] = eg_part(cc, n).astype(BF)
            ya_copy(cc, n).start()
        yown[cc] = eg_part(cc, 0)

    def conv_grad(a, _):
        hg = dot(wv[pl.ds(4 * a, 4)].reshape(512, 1024), tgo[...], NT)
        pg = (hg * dgelu[pl.ds(4 * a, 4)].reshape(512, 256)).astype(BF)
        for da in range(3):
            total = cga[da]
            for b in range(4):
                total = total + dot(pg[128 * b : 128 * b + 128], xs[a + da, CP * b : CP * b + 256, :], NT)
            cga[da] = total
        return 0

    lax.fori_loop(0, 4, conv_grad, 0, unroll=4)
    half_o = pl.ds(pl.multiple_of(64 * other, 64), 64)
    q_copy = remote(cga.at[:, half_o, :], cgp, q_s, q_r, lon, lat, other)
    q_copy.start()

    def d_copy(j):
        i = lax.rem(j - lon + 16, 16)
        return remote(scb16.at[j], rcg.at[i], d_s.at[j], d_r.at[i], j, lat, ch)

    def e_copy(i):
        return remote(l0, rl.at[lat], e_s.at[i], e_r.at[i], lon, lax.rem(lat + i, 8), ch)

    def f_copy(i):
        return remote(l1, agb.at[lon], f_s.at[i], f_r.at[lon], lax.rem(lon + i, 16), lat, ch)

    q_copy.wait_recv()
    total = cga[:, pl.ds(pl.multiple_of(64 * ch, 64), 64), :] + cgp[...]
    for j in range(12):
        for half in range(2):
            piece = total[j // 4, 16 * (j % 4) : 16 * (j % 4) + 16, 128 * half : 128 * half + 128]
            scg[j, half] = piece
            scb16[j, half] = piece.astype(BF)
    for j in range(12):

        @pl.when(j != lon)
        def _(j=j):
            d_copy(j).start()

    stage_xb(0)
    stage_yb(0)
    stage_xb(1)
    stage_yb(1)

    @pl.when(lon < 12)
    def _():
        total = scg[lon]
        for i in range(1, 16):
            remote(scb16.at[0], rcg.at[i], d_s.at[0], d_r.at[i], lon, lat, other).wait_recv()
            total = total + rcg[i].astype(F32)
        l0[...] = total
        rl[lat] = total
        for i in range(1, 8):
            e_copy(i).start()

    stage_c(0)
    stage_c(2)
    stage_c(1)

    @pl.when(lon < 12)
    def _():
        for i in range(1, 8):
            e_copy(i).wait_recv()
        total = rl[0]
        for i in range(1, 8):
            total = total + rl[i]
        total = total.astype(BF)
        l1[...] = total
        agb[lon] = total
        for i in range(1, 16):
            f_copy(i).start()

    stage_c(3)
    total = scf[lon]
    for i in range(1, 16):
        remote(scb.at[0], rc.at[i], c_s.at[i], c_r.at[i], lon, lat, other).wait_recv()
        total = total + rc[i].astype(F32)
    eg_out[...] = total

    for j in range(12):

        @pl.when(j != lon)
        def _(j=j):
            remote(l1, agb.at[j], f_s.at[0], f_r.at[j], lon, lat, other).wait_recv()

        for half in range(2):
            full[j // 4, 16 * (j % 4) : 16 * (j % 4) + 16, 128 * half : 128 * half + 128] = agb[j, half].astype(F32)
    for da in range(3):
        for db in range(3):
            cg_out[3 * da + db] = full[da, :, CP * db : CP * db + 69]

    for i in range(8):
        for g in range(2):
            remote(
                emb.at[0, pl.ds(0, 32)], emb_out.at[pl.ds(0, 32)],
                em_s.at[0], em_r.at[2 * i + g], lon, lat, other,
            ).wait_recv()

    @pl.when(has_inner)
    def _():
        for c in inner:
            c.wait_send()

    @pl.when(has_polar)
    def _():
        for c in polar_s:
            c.wait_send()

    wc_remote.wait_send()
    for i in range(1, 8):
        tg_copies[i].wait_send()

    @pl.when(ch != hi)
    def _():
        tg_copies[0].wait_send()

    pk0.wait_send()
    pk1.wait_send()
    hp.wait_send()
    q_copy.wait_send()
    for c in forwards:
        c.wait_send()
    for (i, g), c in emb_copies.items():
        if i:
            c.wait_send()
        else:

            @pl.when(jnp.logical_not((ch == hi) & (ch == g)))
            def _(c=c):
                c.wait_send()

    for cc in range(2):
        for n in (1, 2, 3):
            ya_copy(cc, n).wait_send()
            xb_copy(cc, n).wait_send()
        yb_copy(cc).wait_send()
        xa_copy(cc).wait_send()
    for i in range(1, 16):
        remote(scb.at[0], rc.at[i], c_s.at[i], c_r.at[i], lon, lat, other).wait_send()
    for j in range(12):

        @pl.when(j != lon)
        def _(j=j):
            d_copy(j).wait_send()

    @pl.when(lon < 12)
    def _():
        for i in range(1, 16):
            f_copy(i).wait_send()
        for i in range(1, 8):
            e_copy(i).wait_send()


def step(t, wc, w, tg):
    vm = pltpu.VMEM
    sem = pltpu.SemaphoreType.DMA
    scratch = [
        vm((69, 64, 128), BF), vm((64 * CP, 128), F32), vm((CP, 128), BF), vm((34, CP, 128), BF), vm((CP, 128), BF), vm((CP, 128), BF), vm((CP, 128), BF), vm((CP, 128), BF),
        vm((CP, 128), BF), vm((CP, 128), BF),
        vm((3, 128, 256), BF), vm((16, 128, 1024), BF), vm((256, 1024), BF), vm((256, 1024), BF),
        vm((6, 2 * CP, 512), BF), vm((512, 768), BF), vm((6, 496, 256), BF),
        vm((16, 2, 64, 256), BF), vm((16, 64, 256), BF), vm((256, 2048), BF), vm((16, 128, 256), F32),
        vm((2, 256, 512), BF),
        vm((2, 3, 256, 256), BF), vm((2, 3, 256, 256), BF), vm((2, 256, 256), F32),
        vm((2, 256, 128), BF), vm((2, 256, 128), BF), vm((2, 256, 128), F32),
        vm((2, 256, 512), BF), vm((2, 256, 512), BF), vm((2, 256, 512), F32),
        vm((2, 3, 256, 128), BF), vm((2, 3, 256, 128), BF), vm((2, 256, 128), F32),
        vm((16, 64, 128), F32), vm((16, 64, 128), BF), vm((16, 64, 128), BF),
        vm((3, 128, 256), F32), vm((3, 64, 256), F32), vm((12, 2, 16, 128), F32), vm((12, 2, 16, 128), BF),
        vm((16, 2, 16, 128), BF), vm((2, 16, 128), F32), vm((8, 2, 16, 128), F32), vm((2, 16, 128), BF),
        vm((12, 2, 16, 128), BF), vm((3, 64, 256), F32),
        sem((18,)), sem((8,)), sem((8,)), sem((6,)), sem((3,)), sem((2,)), sem((2,)), sem, sem,
        sem((16,)), sem((16,)), sem((8,)), sem((8,)), sem, sem,
        sem((2, 3)), sem((2, 3)), sem((2,)), sem((2,)), sem((2,)), sem((2,)), sem((2, 3)), sem((2, 3)), sem((16,)), sem((16,)), sem, sem,
        sem((12,)), sem((16,)), sem((8,)), sem((8,)), sem((16,)), sem((12,)),
    ]
    any_ = pl.BlockSpec(memory_space=pl.ANY)
    inside = pl.BlockSpec(memory_space=pltpu.VMEM)
    return pl.pallas_call(
        kernel,
        out_shape=(
            jax.ShapeDtypeStruct((512, 512), BF),
            jax.ShapeDtypeStruct((64, 128), F32),
            jax.ShapeDtypeStruct((9, 64, 69), F32),
        ),
        in_specs=[any_, inside, any_, any_],
        out_specs=(any_, inside, inside),
        scratch_shapes=scratch,
        compiler_params=pltpu.CompilerParams(vmem_limit_bytes=56 * 1024 * 1024, has_side_effects=True, collective_id=0),
    )(t, wc, w, tg)


def settle(emb, eg, cg, emb_out, eg_out, cg_out, emb_held, eg_held, cg_held, sem):
    moves = []
    for n in range(4):
        rows = pl.ds(128 * n, 128)
        moves.append((emb.at[rows], emb_held.at[rows], emb_out.at[rows]))
    moves += [(eg, eg_held, eg_out), (cg, cg_held, cg_out)]
    moves = [
        (pltpu.make_async_copy(a, b, sem.at[0, n]), pltpu.make_async_copy(b, c, sem.at[1, n]))
        for n, (a, b, c) in enumerate(moves)
    ]
    for first, _ in moves:
        first.start()
    for first, second in moves:
        first.wait()
        second.start()
    for _, second in moves:
        second.wait()


def body(fields, conv_weight, embed_weight, token_grads):
    embedded, embed_gradient, conv_gradient = step(fields, conv_weight.transpose(1, 0, 2), embed_weight, token_grads.reshape(512, 1024))
    shapes = [(a.shape, a.dtype) for a in (embedded, embed_gradient, conv_gradient)]
    outside = pl.BlockSpec(memory_space=pltpu.HBM)
    embedded, embed_gradient, conv_gradient = pl.pallas_call(
        settle,
        out_shape=tuple(jax.ShapeDtypeStruct(*a) for a in shapes),
        in_specs=[outside] * 3,
        out_specs=(outside,) * 3,
        scratch_shapes=[pltpu.VMEM(*a) for a in shapes] + [pltpu.SemaphoreType.DMA((2, 6))],
    )(embedded, embed_gradient, conv_gradient)
    return embedded.reshape(1, 1, 512, 512), conv_gradient.transpose(1, 0, 2), embed_gradient


def solution(mesh):
    return jax.shard_map(
        body,
        mesh=mesh,
        in_specs=(P(None, "lat", "lon"), P("ch", None, None), P(), P("lon", "lat", None, None)),
        out_specs=(P("lon", "lat", None, "ch"), P("ch", None, None), P("ch", ("lon", "lat"))),
        check_vma=False,
    )
```
